512 devices in a mesh: tile: 64 (over y, x, core), chan: 8 (over z).
Axes of the slice: x: 4, y: 8, z: 8, core: 2. Of those that a mesh axis runs over, the one named last changes fastest.
Arguments:
- activations: bfloat16 [64, 128, 4096], P('tile', 'chan'), may hold values from -6 to 6
- cotangent: bfloat16 [64, 128, 4096], P('tile', 'chan'), may hold values from -6 to 6
- kernel: float32 [128, 49], P('chan'), may hold values from -0.875 to 0.875
- gain: float32 [128], replicated, may hold values from 0.25 to 2
- w_in: bfloat16 [128, 512], P(None, 'chan'), may hold values from -0.5 to 0.5
- w_out: bfloat16 [512, 128], P('chan'), may hold values from -0.25 to 0.25
- neighbours: int32 [64, 8], P('tile'), may hold values from -1 to 63, as said below
- land_mask: int32 [64, 4096], P('tile'), may hold values 0 or 1
Outputs:
- output: bfloat16 [64, 128, 4096], P('tile', 'chan')
- input_grad: bfloat16 [64, 128, 4096], P('tile', 'chan')
- kernel_grad: float32 [128, 49], P('chan')
- gain_grad: float32 [128], P('chan')
- w_in_grad: float32 [128, 512], P(None, 'chan')
- w_out_grad: float32 [512, 128], P('chan')
The draws below stay inside these ranges and needn't reach their ends.
Inputs may be any that keep to these rules, and one draw needn't show every extreme that they name: neighbours[s, k] is the ocean tile beside tile s in direction k, tiles lying on a grid whose columns wrap around and whose top and bottom rows have nothing beyond; -1 for land or beyond the grid; if t is beside s in one direction then s is beside t in the opposite one.
All inputs are finite; a program needn't handle non-finite values. No bound on the sum of `land_mask` on one device may be relied on, other than what follows from the above.
Results may differ from the reference program's by a relative error of at most 0.019.
Values may be sent and summed in bfloat16 or wider, within the bound.
A program may use at most 64 MiB of HBM per device.

```python
import math
import jax
import jax.numpy as jnp
from jax import lax

C = 128
HID = 512
SIDE = 64
TILES = 64
N_CHAN = 8


OFFSETS = ((-1, -1), (-1, 0), (-1, 1), (0, -1), (0, 1), (1, -1), (1, 0), (1, 1))


def draw_neighbours(key, part):
    key = jax.random.fold_in(key, 11)
    spots = TILES + TILES // 2
    height = spots // 8
    order = jax.random.permutation(key, spots).astype(jnp.int32)
    ocean = order[:TILES]
    owner = jnp.full((spots,), -1, jnp.int32).at[ocean].set(jnp.arange(TILES, dtype=jnp.int32))
    rows = ocean // 8
    cols = ocean % 8
    found = []
    for step_row, step_col in OFFSETS:
        near_row = rows + step_row
        near_col = (cols + step_col) % 8
        inside = (near_row >= 0) & (near_row < height)
        place = jnp.clip(near_row, 0, height - 1) * 8 + near_col
        found.append(jnp.where(inside, owner[place], -1))
    return jnp.stack(found, 1).astype(jnp.int32)


def set_ends(values, rng, low, high):
    spot = [jax.random.randint(jax.random.fold_in(rng, axis), (), 0, length) for axis, length in enumerate(values.shape)]
    main_axis = values.shape.index(max(values.shape))
    neighbour = spot[:main_axis] + [(spot[main_axis] + 1) % values.shape[main_axis]] + spot[main_axis + 1:]
    return values.at[tuple(spot)].set(low).at[tuple(neighbour)].set(high)


def shard_levels(key, dims, split, least, high):
    level, own = 1.0, jax.random.fold_in(key, 6)
    for dim, shards_of in split:
        heights = jnp.exp(jax.random.uniform(jax.random.fold_in(own, dim), (shards_of,), jnp.float32, least / len(split), high / len(split)))
        level = level * jnp.repeat(heights, dims[dim] // shards_of).reshape([-1 if axis == dim else 1 for axis in range(len(dims))])
    return level


def scatter_about(key, dims, deviation, reach, split=(), held_as=jnp.bfloat16):
    level = shard_levels(key, dims, split, -0.22, 0.18) if split else 1.0
    result = jax.random.normal(key, dims, jnp.float32) * deviation * level
    return jnp.minimum(jnp.maximum(result, -reach), reach).astype(held_as)


def setup_inputs(seed: int = 0) -> dict:
    key_list = jax.random.split(jax.random.key(seed), 9)
    return {
        "activations": scatter_about(key_list[0], (TILES, C, SIDE * SIDE), 1.0, 6.0, ((0, 64), (1, 8))),
        "cotangent": scatter_about(key_list[1], (TILES, C, SIDE * SIDE), 1.0, 6.0, ((0, 64), (1, 8))),
        "kernel": scatter_about(key_list[2], (C, 49), 49 ** -0.5, 0.875, ((0, 8),), jnp.float32),
        "gain": jnp.clip(jnp.exp(jax.random.uniform(key_list[3], (C,), jnp.float32, math.log(0.25), math.log(2.0))), 0.25, 2.0),
        "w_in": scatter_about(key_list[4], (C, HID), C ** -0.5, 0.5, ((1, 8),)),
        "w_out": scatter_about(key_list[5], (HID, C), HID ** -0.5, 0.25, ((0, 8),)),
        "neighbours": draw_neighbours(jax.random.fold_in(key_list[8], 71), 0),
        "land_mask": set_ends((jax.random.randint(key_list[7], (TILES, SIDE * SIDE), 0, 5) < 4).astype(jnp.int32), jax.random.fold_in(key_list[7], 1), 0, 1),
    }


EPS = 1e-06

def rim_strips(grid):
    count, chans, side, _ = grid.shape
    top = grid[:, :, :3, :]
    bottom = grid[:, :, side - 3:, :]
    left = jnp.swapaxes(grid[:, :, :, :3], 2, 3)
    right = jnp.swapaxes(grid[:, :, :, side - 3:], 2, 3)
    return jnp.stack([top, bottom, left, right], 2).reshape(count, chans, 12 * side)

def assemble(center, near):
    side = center.shape[-1]
    above = near[:, 0:3, :, 1]
    below = near[:, 5:8, :, 0]
    west = jnp.swapaxes(near[:, 3, :, 3], 2, 3)
    east = jnp.swapaxes(near[:, 4, :, 2], 2, 3)
    top_row = jnp.concatenate([above[:, 0, :, :, side - 3:], above[:, 1], above[:, 2, :, :, :3]], -1)
    middle = jnp.concatenate([west, center, east], -1)
    bottom_row = jnp.concatenate([below[:, 0, :, :, side - 3:], below[:, 1], below[:, 2, :, :, :3]], -1)
    return jnp.concatenate([top_row, middle, bottom_row], 2)

def depthwise(padded, kernel):
    side = padded.shape[-1] - 6
    total = jnp.zeros(padded.shape[:2] + (side, side), jnp.float32)
    for row in range(7):
        for col in range(7):
            total = total + kernel[None, :, row * 7 + col, None, None] * padded[:, :, row:row + side, col:col + side].astype(jnp.float32)
    return total

def flipped(padded, kernel):
    side = padded.shape[-1] - 6
    total = jnp.zeros(padded.shape[:2] + (side, side), jnp.float32)
    for row in range(7):
        for col in range(7):
            total = total + kernel[None, :, row * 7 + col, None, None] * padded[:, :, 6 - row:6 - row + side, 6 - col:6 - col + side].astype(jnp.float32)
    return total

def kernel_grad_of(padded, grads):
    side = grads.shape[-1]
    weights = grads.astype(jnp.float32)
    columns = []
    for row in range(7):
        for col in range(7):
            columns.append(lax.optimization_barrier(jnp.sum(weights * padded[:, :, row:row + side, col:col + side].astype(jnp.float32), axis=(0, 2, 3))))
    return jnp.stack(columns, 1)

def gelu_pair(pre):
    inner = 0.7978845608 * (pre + 0.044715 * pre * pre * pre)
    bend = jnp.tanh(inner)
    value = 0.5 * pre * (1.0 + bend)
    slope = 0.5 * (1.0 + bend) + 0.5 * pre * (1.0 - bend * bend) * 0.7978845608 * (1.0 + 3.0 * 0.044715 * pre * pre)
    return (value, slope)

def sum_by_group(parts):
    rounded = lax.optimization_barrier(parts.astype(jnp.bfloat16))
    return lax.optimization_barrier(jnp.sum(rounded.astype(jnp.float32), 0))

def reference(activations, cotangent, kernel, gain, w_in, w_out, neighbours, land_mask):
    tiles, chans, cells = activations.shape
    side = SIDE
    groups = N_CHAN
    width = HID // groups
    grid = activations.reshape(tiles, chans, side, side)
    slots = jnp.where(neighbours < 0, tiles, neighbours).astype(jnp.int32)
    table = jnp.concatenate([rim_strips(grid), jnp.zeros((1, chans, 12 * side), jnp.bfloat16)], 0)
    output_groupings = w_out.reshape(groups, width, chans).astype(jnp.float32)
    input_groupings = w_in.reshape(chans, groups, width).astype(jnp.float32)

    def first_pass(index):
        center = grid[index][None]
        near = table[slots[index]].reshape(1, 8, chans, 4, 3, side)
        padded = assemble(center, near)
        conv = depthwise(padded, kernel)[0].reshape(chans, cells)
        mean = lax.optimization_barrier(jnp.sum(conv, 0)) / chans
        meansq = lax.optimization_barrier(jnp.sum(conv * conv, 0)) / chans
        rstd = lax.rsqrt(meansq - mean * mean + EPS)
        normed = (conv - mean) * rstd
        feats = (normed * gain[:, None]).astype(jnp.bfloat16)
        pre = jnp.dot(w_in.T, feats, preferred_element_type=jnp.float32)
        value, slope = gelu_pair(pre)
        act = value.astype(jnp.bfloat16)
        activation_groupings = act.reshape(groups, width, cells).astype(jnp.float32)
        residual_branch = sum_by_group(jnp.einsum('izy,izj->iyj', output_groupings, activation_groupings))
        mask = land_mask[index].astype(jnp.float32)
        out = (activations[index].astype(jnp.float32) + mask * residual_branch).astype(jnp.bfloat16)
        masked = (cotangent[index].astype(jnp.float32) * mask).astype(jnp.bfloat16)
        grad_out = jnp.dot(act, masked.T, preferred_element_type=jnp.float32)
        d_act = jnp.dot(w_out, masked, preferred_element_type=jnp.float32)
        d_pre = (d_act * slope).astype(jnp.bfloat16)
        grad_in = jnp.dot(feats, d_pre.T, preferred_element_type=jnp.float32)
        preactivation_groupings = d_pre.reshape(groups, width, cells).astype(jnp.float32)
        feature_cotangent = sum_by_group(jnp.einsum('lhm,hmx->hlx', input_groupings, preactivation_groupings))
        grad_gain = lax.optimization_barrier(jnp.sum(feature_cotangent * normed, 1))
        d_norm = feature_cotangent * gain[:, None]
        first = lax.optimization_barrier(jnp.sum(d_norm, 0)) / chans
        second = lax.optimization_barrier(jnp.sum(d_norm * normed, 0)) / chans
        d_conv = (rstd * (d_norm - first - normed * second)).astype(jnp.bfloat16)
        grad_kernel = kernel_grad_of(padded, d_conv.reshape(1, chans, side, side))
        return (out, d_conv, grad_in, grad_out, grad_gain, grad_kernel)
    order = jnp.arange(tiles, dtype=jnp.int32)
    out, d_conv, grad_in, grad_out, grad_gain, grad_kernel = lax.map(first_pass, order)
    dgrid = d_conv.reshape(tiles, chans, side, side)
    dtable = jnp.concatenate([rim_strips(dgrid), jnp.zeros((1, chans, 12 * side), jnp.bfloat16)], 0)

    def second_pass(index):
        near = dtable[slots[index]].reshape(1, 8, chans, 4, 3, side)
        padded = assemble(dgrid[index][None], near)
        back = flipped(padded, kernel)[0].reshape(chans, cells)
        return (cotangent[index].astype(jnp.float32) + back).astype(jnp.bfloat16)
    input_grad = lax.map(second_pass, order)
    return (out, input_grad, lax.optimization_barrier(jnp.sum(grad_kernel, 0)), lax.optimization_barrier(jnp.sum(grad_gain, 0)), lax.optimization_barrier(jnp.sum(grad_in, 0)), lax.optimization_barrier(jnp.sum(grad_out, 0)))
```

```python
import jax
import jax.numpy as jnp
from jax import lax
from jax.experimental import pallas as pl
from jax.experimental.pallas import tpu as pltpu
from jax.sharding import PartitionSpec as P

EPS = 1e-06
N = 8
F32 = jnp.float32
BF16 = jnp.bfloat16

(RIM_Y, RIM_X, DRIM_Y, DRIM_X, WEIGHTS, MASKED, CONV, MEANS, DCONV, BRANCH, GAIN, G_X, G_Z, G_Y, G_ALL, S_Y, S_X) = range(17)


def dot(a, b, dims):
    return lax.dot_general(a, b, (dims, ((), ())), preferred_element_type=F32)


def lanes(t, width=128):
    return pl.ds(pl.multiple_of(t * width, width), width)


def rows16(p):
    return pl.ds(pl.multiple_of(p * 16, 16), 16)


def kernel_body(
    act, cot, ker, gain, w_in, w_out, nbr, mask,
    out, igrad, small_out, wgrad_out,
    xpad, dpad, wb, rim, drim, table, dtable, masks, hsend, dhsend, hbuf, dhbuf,
    weights, masked, conv_r, means, convs, mean_all, dz, normed, feats, act_h, dpre_h,
    dconv_s, dconv, branch_s, branch, gain_s, gains, g_s, g_x, g_xs, g_z, g_y, g_all, s_y, s_x,
    ssem, rsem,
):
    tile = lax.axis_index("tile")
    z = lax.axis_index("chan")
    y = tile // N
    q = lax.rem(tile, N)
    mine = {"y": y, "x": q, "z": z}

    def device(group, p):
        if group == "y":
            return (p * N + q, z)
        if group == "x":
            return (y * N + p, z)
        return (tile, p)

    def copy(stage, group, src, dst, to, slot):
        return pltpu.make_async_remote_copy(
            src_ref=src,
            dst_ref=dst,
            send_sem=ssem.at[stage, to],
            recv_sem=rsem.at[stage, slot],
            device_id=device(group, to),
            device_id_type=pl.DeviceIdType.MESH,
        )

    def peers(group, step):
        def one(j, carry):
            step(lax.rem(mine[group] + j, N))
            return carry

        lax.fori_loop(1, N, one, 0)

    sent = []

    def start(stage, group, src, dst):
        me = mine[group]
        peers(group, lambda p: copy(stage, group, src(p), dst(me), p, me).start())
        sent.append((stage, group, src, dst))

    def arrive(stage, group, src, dst):
        peers(group, lambda p: copy(stage, group, src(p), dst(p), p, p).wait_recv())

    lane = lax.broadcasted_iota(jnp.int32, (16, 128), 1)
    lane1 = lax.broadcasted_iota(jnp.int32, (1, 1, 128), 2)
    low = lane < 64
    rest = lane & 63
    edge = (rest < 3) | (rest >= 61)
    beside = ((lane >= 64) & (lane < 67)) | (lane >= 125)

    def window_in(index, members):
        found = index < 0
        for member in members:
            found = found | (index == member)
        return found

    def pair(ref, t):
        return ref[:, lanes(t)].astype(F32)

    def roll(x, shift, axis):
        shift = shift % 128
        return x if shift == 0 else pltpu.roll(x, shift, axis)

    barrier = pltpu.get_barrier_semaphore()
    for group in ("y", "x", "z"):
        peers(
            group,
            lambda p, group=group: pl.semaphore_signal(
                barrier, inc=1, device_id=device(group, p), device_id_type=pl.DeviceIdType.MESH
            ),
        )

    def build_rim(src, dst):
        first = src[:, 0:128]
        dst[0:16, :] = first
        dst[16:32, :] = jnp.where(low, pair(src, 1), pair(src, 30)).astype(BF16)
        dst[32:48, :] = src[:, 3968:4096]

        def pack(block, carry):
            total = jnp.zeros((16, 128), F32)
            for t in range(8):
                total = total + roll(jnp.where(edge, pair(src, block * 8 + t), 0.0), 8 * t, 1)
            dst[rows16(3 + block), :] = total.astype(BF16)
            return carry

        lax.fori_loop(0, 4, pack, 0)

    build_rim(act, rim)
    list_row = lax.broadcasted_iota(jnp.int32, (16, 128), 0)
    listed = jnp.full((16, 128), -1.0, F32)
    for k in range(8):
        listed = jnp.where(list_row == k, nbr[0, k].astype(F32), listed)
    rim[112:128, :] = listed.astype(BF16)

    pl.semaphore_wait(barrier, 3 * (N - 1))
    rim_src, rim_dst = (lambda p: rim), (lambda p: table.at[p])
    start(RIM_Y, "y", rim_src, rim_dst)

    eye = (
        lax.broadcasted_iota(jnp.int32, (64, 64), 0) == lax.broadcasted_iota(jnp.int32, (64, 64), 1)
    ).astype(BF16)
    weights[z, 0:64, :] = dot(eye, w_in[...], ((1,), (1,))).astype(BF16)
    weights[z, 64:128, :] = w_out[...]
    w_src, w_dst = (lambda p: weights.at[z]), (lambda p: weights.at[p])
    start(WEIGHTS, "z", w_src, w_dst)

    def mask_cot(t, carry):
        kept = mask[:, lanes(t, 512)].astype(F32)
        masked[:, lanes(t, 512)] = (cot[:, lanes(t, 512)].astype(F32) * kept).astype(BF16)
        return carry

    lax.fori_loop(0, 8, mask_cot, 0)
    m_src, m_dst = (lambda p: masked.at[:, lanes(p, 512)]), (lambda p: dz.at[rows16(p), :])
    start(MASKED, "z", m_src, m_dst)
    dz[rows16(z), :] = masked[:, lanes(z, 512)]

    for tap in range(49):
        wb[tap] = jnp.broadcast_to(ker[:, tap : tap + 1], (16, 128))

    def spread(src, dst):
        def rows(t, carry):
            both = pair(src, t)
            dst[3 + 2 * t] = jnp.where(low, both, 0.0)
            dst[4 + 2 * t] = jnp.where(low, roll(both, 64, 1), 0.0)
            return carry

        lax.fori_loop(0, 32, rows, 0)

    spread(act, xpad)

    index4 = lane1 // 4
    odd = (index4 & 1) == 1
    in_top = window_in(index4, (0, 15, 16, 31, 2, 17))
    in_bottom = window_in(index4, (28, 11, 14, 29, 30, 13))
    table_own = table.at[y]
    table_own[...] = rim[...]
    arrive(RIM_Y, "y", rim_src, rim_dst)

    def make_masks(d, carry):
        number = (y * N + d).astype(F32)
        near = (table[:, 112:128, :].astype(F32) == number).astype(F32)
        m = [near[:, k : k + 1, :] for k in range(8)]
        masks[d, :, 0:1, :] = m[1]
        masks[d, :, 1:2, :] = jnp.where(lane1 < 64, m[1], m[6])
        masks[d, :, 2:3, :] = m[6]
        masks[d, :, 3:4, :] = jnp.where(odd, m[4], m[3])
        masks[d, :, 4:5, :] = jnp.where(
            in_top, jnp.where(odd, m[2], m[0]), jnp.where(in_bottom, jnp.where(odd, m[7], m[5]), 0.0)
        )
        return carry

    lax.fori_loop(0, N, make_masks, 0)

    def choose(src, dst):
        def one(d, carry):
            for part in range(8):
                if part < 7:
                    block = src[:, 16 * part : 16 * part + 16, :].astype(F32)
                else:
                    block = jnp.where(
                        in_bottom, src[:, 96:112, :].astype(F32), src[:, 48:64, :].astype(F32)
                    )
                kind = part if part < 3 else 3 if part < 7 else 4
                total = jnp.sum(masks[d, :, kind : kind + 1, :] * block, 0)
                dst[d, 16 * part : 16 * part + 16, :] = total.astype(BF16)
            return carry

        lax.fori_loop(0, N, one, 0)

    def finish_halo(own, got, dst):
        def part(i):
            total = own[q, 16 * i : 16 * i + 16, :].astype(F32)
            for j in range(1, N):
                total = total + got[lax.rem(q + j, N), 16 * i : 16 * i + 16, :].astype(F32)
            return total

        top, mid, end, corner = part(0), part(1), part(2), part(7)

        def outer(row, center, shift):
            dst[row] = jnp.where(low, center, jnp.where(beside, roll(corner, shift, 1), 0.0))

        outer(67, top, 64)
        outer(68, roll(top, 64, 1), 0)
        outer(69, mid, 56)
        outer(0, roll(mid, 64, 1), 80)
        outer(1, end, 8)
        outer(2, roll(end, 64, 1), 72)
        for block in range(4):
            cols = part(3 + block)
            for t in range(8):
                for o in range(2):
                    row = 3 + 16 * block + 2 * t + o
                    near = roll(cols, 64 * (1 - o) - 8 * t, 1)
                    dst[row] = dst[row] + jnp.where(beside, near, 0.0)

    choose(table, hsend)
    h_src, h_dst = (lambda p: hsend.at[p]), (lambda p: hbuf.at[p])
    start(RIM_X, "x", h_src, h_dst)
    arrive(RIM_X, "x", h_src, h_dst)
    finish_halo(hsend, hbuf, xpad)

    def filtered(src, flip, r):
        total = None
        for b in range(7):
            part = None
            for a in range(7):
                tap = (6 - a) * 7 + 6 - b if flip else a * 7 + b
                term = wb[tap][None] * src[pl.ds(8 * r + a, 8)]
                part = term if part is None else part + term
            part = roll(part, 3 - b, 2)
            total = part if total is None else total + part
        return [jnp.where(low, total[2 * u], roll(total[2 * u + 1], 64, 1)) for u in range(4)]

    c_src, c_dst = (lambda p: conv_r.at[:, lanes(p, 512)]), (lambda p: convs.at[rows16(p), :])
    a_src, a_dst = (lambda p: means.at[:, lanes(p, 512)]), (lambda p: mean_all.at[p])

    def forward(j, carry):
        r = lax.rem(z + 1 + j, N)
        tiles = filtered(xpad, False, r)
        for u in range(4):
            mean = jnp.sum(tiles[u], 0, keepdims=True) * (1.0 / 16)
            conv_r[:, lanes(4 * r + u)] = (tiles[u] - mean).astype(BF16)
            means[:, lanes(4 * r + u)] = mean

        @pl.when(j < N - 1)
        def _():
            copy(CONV, "z", c_src(r), c_dst(z), r, z).start()
            copy(MEANS, "z", a_src(r), a_dst(z), r, z).start()

        return carry

    lax.fori_loop(0, N, forward, 0)
    sent.append((CONV, "z", c_src, c_dst))
    sent.append((MEANS, "z", a_src, a_dst))
    convs[rows16(z), :] = conv_r[:, lanes(z, 512)]
    mean_all[z] = means[:, lanes(z, 512)]
    arrive(CONV, "z", c_src, c_dst)
    arrive(MEANS, "z", a_src, a_dst)

    local = mean_all[...]
    mean = jnp.sum(local, 0) * (1.0 / N)
    centred = (convs[...].astype(F32).reshape(N, 16, 512) + (local - mean[None])).reshape(128, 512)
    rstd = lax.rsqrt(jnp.sum(centred * centred, 0, keepdims=True) * (1.0 / 128) + EPS)
    normed[...] = centred * rstd
    diagonal = lax.broadcasted_iota(jnp.int32, (128, 128), 0) == lax.broadcasted_iota(
        jnp.int32, (128, 128), 1
    )
    gain_col = jnp.sum(jnp.where(diagonal, jnp.broadcast_to(gain[...], (128, 128)), 0.0), 1, keepdims=True)
    feats[...] = (normed[...] * gain_col).astype(BF16)
    arrive(WEIGHTS, "z", w_src, w_dst)
    arrive(MASKED, "z", m_src, m_dst)

    def hidden(g, carry):
        wi = weights[pl.ds(2 * g, 2), 0:64, :].reshape(128, 128)
        wo = weights[pl.ds(2 * g, 2), 64:128, :].reshape(128, 128)
        pre = dot(wi, feats[...], ((1,), (0,)))
        square = pre * pre
        bend = jnp.tanh(0.7978845608 * pre * (1.0 + 0.044715 * square))
        half = 0.5 + 0.5 * bend
        act_h[lanes(g), :] = (pre * half).astype(BF16)
        slope = half + (0.5 * 0.7978845608) * pre * (1.0 - bend * bend) * (
            1.0 + (3.0 * 0.044715) * square
        )
        d_act = dot(wo, dz[...], ((1,), (0,)))
        dpre_h[lanes(g), :] = (d_act * slope).astype(BF16)
        return carry

    lax.fori_loop(0, 4, hidden, 0)
    wi_all = weights[:, 0:64, :].reshape(512, 128)
    wo_all = weights[:, 64:128, :].reshape(512, 128)
    d_feat = dot(wi_all, dpre_h[...], ((0,), (0,)))
    per_gain = d_feat * normed[...]
    d_norm = d_feat * gain_col
    first = jnp.sum(d_norm, 0, keepdims=True) * (1.0 / 128)
    second = jnp.sum(per_gain * gain_col, 0, keepdims=True) * (1.0 / 128)
    dconv_s[...] = (rstd * (d_norm - first - normed[...] * second)).astype(BF16)
    d_src, d_dst = (lambda p: dconv_s.at[rows16(p), :]), (lambda p: dconv.at[:, lanes(p, 512)])
    start(DCONV, "z", d_src, d_dst)
    dconv[:, lanes(z, 512)] = dconv_s[rows16(z), :]
    folded = per_gain[:, 0:128] + per_gain[:, 128:256] + per_gain[:, 256:384] + per_gain[:, 384:512]
    gain_s[...] = folded.reshape(N, 16, 128)
    n_src, n_dst = (lambda p: gain_s.at[p]), (lambda p: gains.at[p])
    start(GAIN, "z", n_src, n_dst)
    gains[z] = gain_s[z]

    g_s[:, 0:64, :] = dot(dpre_h[...], feats[...], ((1,), (1,))).astype(BF16).reshape(N, 64, 128)
    g_s[:, 64:128, :] = dot(act_h[...], dz[...], ((1,), (1,))).astype(BF16).reshape(N, 64, 128)
    gx_src, gx_dst = (lambda p: g_s.at[:, rows16(p), :]), (lambda p: g_x.at[p])
    start(G_X, "x", gx_src, gx_dst)
    branch_s[...] = dot(wo_all, act_h[...], ((0,), (0,))).astype(BF16)
    b_src, b_dst = (lambda p: branch_s.at[rows16(p), :]), (lambda p: branch.at[:, lanes(p, 512)])
    start(BRANCH, "z", b_src, b_dst)
    branch[:, lanes(z, 512)] = branch_s[rows16(z), :]

    arrive(DCONV, "z", d_src, d_dst)
    build_rim(dconv, drim)
    e_src, e_dst = (lambda p: drim), (lambda p: dtable.at[p])
    start(DRIM_Y, "y", e_src, e_dst)
    dtable[y] = drim[...]
    spread(dconv, dpad)

    arrive(G_X, "x", gx_src, gx_dst)
    g_x[q] = g_s[:, rows16(q), :]
    g_xs[...] = jnp.sum(g_x[...].astype(F32), 0)
    gz_src, gz_dst = (lambda p: g_xs.at[p]), (lambda p: g_z.at[p])
    start(G_Z, "z", gz_src, gz_dst)
    g_z[z] = g_xs[z]

    small = jnp.zeros((16, 128), F32)
    for b in range(7):

        def taps(r, carry, b=b):
            moved = roll(dpad[pl.ds(3 + 8 * r, 8)], b - 3, 2)
            return tuple(
                carry[a] + jnp.sum(moved * xpad[pl.ds(8 * r + a, 8)], 0) for a in range(7)
            )

        column = lax.fori_loop(0, 8, taps, tuple(jnp.zeros((16, 128), F32) for _ in range(7)))
        for a in range(7):
            small = jnp.where(lane == a * 7 + b, jnp.sum(column[a], 1, keepdims=True), small)
    arrive(GAIN, "z", n_src, n_dst)
    small = jnp.where(lane == 49, jnp.sum(jnp.sum(gains[...], 0), 1, keepdims=True), small)
    s_y[y] = small
    sy_src, sy_dst = (lambda p: s_y.at[y]), (lambda p: s_y.at[p])
    start(S_Y, "y", sy_src, sy_dst)

    arrive(DRIM_Y, "y", e_src, e_dst)
    choose(dtable, dhsend)
    f_src, f_dst = (lambda p: dhsend.at[p]), (lambda p: dhbuf.at[p])
    start(DRIM_X, "x", f_src, f_dst)

    arrive(G_Z, "z", gz_src, gz_dst)
    g_y[y] = jnp.sum(g_z[...], 0)
    gy_src, gy_dst = (lambda p: g_y.at[y]), (lambda p: g_y.at[p])
    start(G_Y, "y", gy_src, gy_dst)

    arrive(BRANCH, "z", b_src, b_dst)

    def write_out(t, carry):
        at = lanes(t, 512)
        kept = mask[:, at].astype(F32)
        out[:, at] = (act[:, at].astype(F32) + kept * branch[:, at].astype(F32)).astype(BF16)
        return carry

    lax.fori_loop(0, 8, write_out, 0)

    arrive(S_Y, "y", sy_src, sy_dst)
    s_x[q] = jnp.sum(s_y[...], 0)
    sx_src, sx_dst = (lambda p: s_x.at[q]), (lambda p: s_x.at[p])
    start(S_X, "x", sx_src, sx_dst)
    arrive(G_Y, "y", gy_src, gy_dst)
    g_all[q] = jnp.sum(g_y[...], 0)
    ga_src, ga_dst = (lambda p: g_all.at[q]), (lambda p: g_all.at[p])
    start(G_ALL, "x", ga_src, ga_dst)

    arrive(DRIM_X, "x", f_src, f_dst)
    finish_halo(dhsend, dhbuf, dpad)

    def backward(r, carry):
        tiles = filtered(dpad, True, r)
        for u in range(4):
            at = lanes(4 * r + u)
            igrad[:, at] = (cot[:, at].astype(F32) + tiles[u]).astype(BF16)
        return carry

    lax.fori_loop(0, N, backward, 0)

    arrive(S_X, "x", sx_src, sx_dst)
    small_out[...] = jnp.sum(s_x[...], 0)
    arrive(G_ALL, "x", ga_src, ga_dst)
    wgrad_out[...] = g_all[...].reshape(128, 128)
    for stage, group, src, dst in sent:
        me = mine[group]
        peers(group, lambda p: copy(stage, group, src(p), dst(me), p, me).wait_send())


def body(activations, cotangent, kernel, gain, w_in, w_out, neighbours, land_mask):
    vmem = pl.BlockSpec(memory_space=pltpu.VMEM)
    smem = pl.BlockSpec(memory_space=pltpu.SMEM)
    scratch = [
        ((70, 16, 128), F32),
        ((70, 16, 128), F32),
        ((49, 16, 128), F32),
        ((128, 128), BF16),
        ((128, 128), BF16),
        ((N, 128, 128), BF16),
        ((N, 128, 128), BF16),
        ((N, N, 8, 128), F32),
        ((N, 128, 128), BF16),
        ((N, 128, 128), BF16),
        ((N, 128, 128), BF16),
        ((N, 128, 128), BF16),
        ((N, 128, 128), BF16),
        ((16, 4096), BF16),
        ((16, 4096), BF16),
        ((1, 4096), F32),
        ((128, 512), BF16),
        ((N, 1, 512), F32),
        ((128, 512), BF16),
        ((128, 512), F32),
        ((128, 512), BF16),
        ((512, 512), BF16),
        ((512, 512), BF16),
        ((128, 512), BF16),
        ((16, 4096), BF16),
        ((128, 512), BF16),
        ((16, 4096), BF16),
        ((N, 16, 128), F32),
        ((N, 16, 128), F32),
        ((N, 128, 128), BF16),
        ((N, N, 16, 128), BF16),
        ((N, 16, 128), F32),
        ((N, 16, 128), F32),
        ((N, 16, 128), F32),
        ((N, 16, 128), F32),
        ((N, 16, 128), F32),
        ((N, 16, 128), F32),
    ]
    out, igrad, small, wgrad = pl.pallas_call(
        kernel_body,
        out_shape=(
            jax.ShapeDtypeStruct((16, 4096), BF16),
            jax.ShapeDtypeStruct((16, 4096), BF16),
            jax.ShapeDtypeStruct((16, 128), F32),
            jax.ShapeDtypeStruct((128, 128), F32),
        ),
        in_specs=[vmem, vmem, vmem, vmem, vmem, vmem, smem, vmem],
        out_specs=[vmem] * 4,
        scratch_shapes=[pltpu.VMEM(shape, kind) for shape, kind in scratch]
        + [pltpu.SemaphoreType.DMA((17, N)), pltpu.SemaphoreType.DMA((17, N))],
        compiler_params=pltpu.CompilerParams(
            collective_id=0, has_side_effects=True, vmem_limit_bytes=40 * 1024 * 1024
        ),
        cost_estimate=pl.CostEstimate(flops=360000000, bytes_accessed=1000000, transcendentals=262144),
        name="block",
    )(
        activations[0], cotangent[0], kernel, gain.reshape(1, 128), w_in, w_out, neighbours, land_mask,
    )
    return (
        out[None],
        igrad[None],
        small[:, :49],
        small[:, 49],
        wgrad[:64].T,
        wgrad[64:],
    )


def solution(mesh):
    placed = (
        P("tile", "chan", None),
        P("tile", "chan", None),
        P("chan", None),
        P(),
        P(None, "chan"),
        P("chan", None),
        P("tile", None),
        P("tile", None),
    )
    return jax.shard_map(
        body,
        mesh=mesh,
        in_specs=placed,
        out_specs=(
            P("tile", "chan", None),
            P("tile", "chan", None),
            P("chan", None),
            P("chan"),
            P(None, "chan"),
            P("chan", None),
        ),
        check_vma=False,
    )
```

```python
import jax
import jax.numpy as jnp
from jax import lax
from jax.experimental import pallas as pl
from jax.experimental.pallas import tpu as pltpu
from jax.sharding import PartitionSpec as P

EPS = 1e-06
N = 8
F32 = jnp.float32
BF16 = jnp.bfloat16
VMEM_LIMIT = 60 * 1024 * 1024

(
    ROWS_X, COLS_Y, ROWS_Y, COLS_X, D_ROWS_X, D_COLS_Y, D_ROWS_Y, D_COLS_X,
    WEIGHTS, MASKED, CONV, MEANS, DCONV, BRANCH, GAIN, G_X, G_Z, G_Y, G_ALL, S_Y, S_X,
) = range(21)


def dot(a, b, dims):
    return lax.dot_general(a, b, (dims, ((), ())), preferred_element_type=F32)


def lanes(t, width=128):
    return pl.ds(pl.multiple_of(t * width, width), width)


def rows16(p):
    return pl.ds(pl.multiple_of(p * 16, 16), 16)


def kernel_body(
    act_h, cot_h, ker_h, gain_h, w_in_h, w_out_h, nbr_h, mask_h,
    out_h, igrad_h, kgrad_h, ggrad_h, w_in_grad_h, w_out_grad_h,
    act, cot, ker, gain, w_in, w_out, nbr, mask,
    out, igrad, kgrad_out, gain_out, w_in_out, w_out_out,
    xpad, dpad, wb, rows, cols, d_rows, d_cols,
    rows_t, cols_t, d_rows_t, d_cols_t, row_masks, col_masks,
    rows_s, cols_s, d_rows_s, d_cols_s, rows_g, cols_g, d_rows_g, d_cols_g,
    weights, masked, conv_r, means, convs, mean_all, dz, normed, feats, act_h2, dpre_h,
    dconv_s, dconv, branch_s, branch, gain_s, gains, g_s, g_x, g_xs, g_z, g_y, g_all, s_y, s_x,
    ssem, rsem, lsem, osem,
):
    tile = lax.axis_index("tile")
    z = lax.axis_index("chan")
    y = tile // N
    q = lax.rem(tile, N)
    mine = {"y": y, "x": q, "z": z}

    def device(group, p):
        if group == "y":
            return (p * N + q, z)
        if group == "x":
            return (y * N + p, z)
        return (tile, p)

    def copy(stage, group, src, dst, to, slot):
        return pltpu.make_async_remote_copy(
            src_ref=src,
            dst_ref=dst,
            send_sem=ssem.at[stage, to],
            recv_sem=rsem.at[stage, slot],
            device_id=device(group, to),
            device_id_type=pl.DeviceIdType.MESH,
        )

    def peers(group, step):
        def one(j, carry):
            step(lax.rem(mine[group] + j, N))
            return carry

        lax.fori_loop(1, N, one, 0)

    sent = []

    def start(stage, group, src, dst):
        me = mine[group]
        peers(group, lambda p: copy(stage, group, src(p), dst(me), p, me).start())
        sent.append((stage, group, src, dst))

    def arrive(stage, group, src, dst):
        peers(group, lambda p: copy(stage, group, src(p), dst(p), p, p).wait_recv())

    lane = lax.broadcasted_iota(jnp.int32, (16, 128), 1)
    lane1 = lax.broadcasted_iota(jnp.int32, (1, 1, 128), 2)
    low = lane < 64
    rest = lane & 63
    edge = (rest < 3) | (rest >= 61)
    beside = ((lane >= 64) & (lane < 67)) | (lane >= 125)

    def window_in(index, members):
        found = index < 0
        for member in members:
            found = found | (index == member)
        return found

    def pair(ref, t):
        return ref[:, lanes(t)].astype(F32)

    def roll(x, shift, axis):
        shift = shift % 128
        return x if shift == 0 else pltpu.roll(x, shift, axis)

    inputs = [
        (act_h, act), (nbr_h, nbr), (cot_h, cot), (mask_h, mask),
        (w_in_h, w_in), (w_out_h, w_out), (ker_h, ker), (gain_h, gain),
    ]
    loads = [pltpu.make_async_copy(src, dst, lsem.at[i]) for i, (src, dst) in enumerate(inputs)]
    for load in loads:
        load.start()
    results = [
        (out, out_h), (igrad, igrad_h), (kgrad_out, kgrad_h), (gain_out, ggrad_h),
        (w_in_out, w_in_grad_h), (w_out_out, w_out_grad_h),
    ]
    stores = [pltpu.make_async_copy(src, dst, osem.at[i]) for i, (src, dst) in enumerate(results)]

    barrier = pltpu.get_barrier_semaphore()
    for group in ("y", "x", "z"):
        peers(
            group,
            lambda p, group=group: pl.semaphore_signal(
                barrier, inc=1, device_id=device(group, p), device_id_type=pl.DeviceIdType.MESH
            ),
        )

    def build_rows(src, dst):
        dst[0:16, :] = src[:, 0:128]
        dst[16:32, :] = jnp.where(low, pair(src, 1), pair(src, 30)).astype(BF16)
        dst[32:48, :] = src[:, 3968:4096]

    def build_cols(src, dst):
        def pack(block, carry):
            total = jnp.zeros((16, 128), F32)
            for t in range(8):
                total = total + roll(jnp.where(edge, pair(src, block * 8 + t), 0.0), 8 * t, 1)
            dst[rows16(block), :] = total.astype(BF16)
            return carry

        lax.fori_loop(0, 4, pack, 0)

    loads[0].wait()
    build_cols(act, cols)
    build_rows(act, rows)
    loads[1].wait()
    eight = lax.broadcasted_iota(jnp.int32, (16, 8), 0) == lax.broadcasted_iota(jnp.int32, (16, 8), 1)
    listed = jnp.sum(
        jnp.where(eight, jnp.broadcast_to(nbr[...].astype(F32), (16, 8)), 0.0), 1, keepdims=True
    )
    listed = jnp.broadcast_to(listed, (16, 128)).astype(BF16)
    rows[48:64, :] = listed
    cols[64:80, :] = listed

    pl.semaphore_wait(barrier, 3 * (N - 1))
    c1_src, c1_dst = (lambda p: cols), (lambda p: cols_t.at[p])
    start(COLS_Y, "y", c1_src, c1_dst)
    r1_src, r1_dst = (lambda p: rows), (lambda p: rows_t.at[p])
    start(ROWS_X, "x", r1_src, r1_dst)
    cols_t[y] = cols[...]
    rows_t[q] = rows[...]

    for load in loads[2:]:
        load.wait()
    weights[z, 0:64, :] = w_in[...]
    weights[z, 64:128, :] = w_out[...]
    w_src, w_dst = (lambda p: weights.at[z]), (lambda p: weights.at[p])
    start(WEIGHTS, "z", w_src, w_dst)

    def mask_cot(t, carry):
        kept = mask[:, lanes(t, 512)].astype(F32)
        masked[:, lanes(t, 512)] = (cot[:, lanes(t, 512)].astype(F32) * kept).astype(BF16)
        return carry

    lax.fori_loop(0, 8, mask_cot, 0)
    m_src, m_dst = (lambda p: masked.at[:, lanes(p, 512)]), (lambda p: dz.at[rows16(p), :])
    start(MASKED, "z", m_src, m_dst)
    dz[rows16(z), :] = masked[:, lanes(z, 512)]

    for tap in range(49):
        wb[tap] = jnp.broadcast_to(ker[:, tap : tap + 1], (16, 128))

    def spread(src, dst):
        def rows(t, carry):
            both = pair(src, t)
            dst[3 + 2 * t] = jnp.where(low, both, 0.0)
            dst[4 + 2 * t] = jnp.where(low, roll(both, 64, 1), 0.0)
            return carry

        lax.fori_loop(0, 32, rows, 0)

    spread(act, xpad)

    index4 = lane1 // 4
    odd = (index4 & 1) == 1
    in_top = window_in(index4, (0, 15, 16, 31, 2, 17))
    in_bottom = window_in(index4, (28, 11, 14, 29, 30, 13))

    def listed_as(table, first, number):
        near = (table[:, first : first + 16, :].astype(F32) == number.astype(F32)).astype(F32)
        return [near[:, k : k + 1, :] for k in range(8)]

    def make_col_masks(d, carry):
        m = listed_as(cols_t, 64, y * N + d)
        col_masks[d, :, 0:1, :] = jnp.where(odd, m[4], m[3])
        col_masks[d, :, 1:2, :] = jnp.where(
            in_top, jnp.where(odd, m[2], m[0]), jnp.where(in_bottom, jnp.where(odd, m[7], m[5]), 0.0)
        )
        return carry

    def make_row_masks(d, carry):
        m = listed_as(rows_t, 48, d * N + q)
        row_masks[d, :, 0:1, :] = m[1]
        row_masks[d, :, 1:2, :] = jnp.where(lane1 < 64, m[1], m[6])
        row_masks[d, :, 2:3, :] = m[6]
        return carry

    def choose_rows(src, dst):
        def one(d, carry):
            for part in range(3):
                block = src[:, 16 * part : 16 * part + 16, :].astype(F32)
                total = jnp.sum(row_masks[d, :, part : part + 1, :] * block, 0)
                dst[d, 16 * part : 16 * part + 16, :] = total.astype(BF16)
            return carry

        lax.fori_loop(0, N, one, 0)

    def choose_cols(src, dst):
        def one(d, carry):
            for part in range(4):
                block = src[:, 16 * part : 16 * part + 16, :].astype(F32)
                total = jnp.sum(col_masks[d, :, 0:1, :] * block, 0)
                dst[d, 16 * part : 16 * part + 16, :] = total.astype(BF16)
            block = jnp.where(in_bottom, src[:, 48:64, :].astype(F32), src[:, 0:16, :].astype(F32))
            dst[d, 64:80, :] = jnp.sum(col_masks[d, :, 1:2, :] * block, 0).astype(BF16)
            return carry

        lax.fori_loop(0, N, one, 0)

    def added(me, own, got, i):
        total = own[me, 16 * i : 16 * i + 16, :].astype(F32)
        for j in range(1, N):
            total = total + got[lax.rem(me + j, N), 16 * i : 16 * i + 16, :].astype(F32)
        return total

    def finish_halo(own_rows, got_rows, own_cols, got_cols, dst):
        top, mid, end = [added(y, own_rows, got_rows, i) for i in range(3)]
        corner = added(q, own_cols, got_cols, 4)

        def outer(row, center, shift):
            dst[row] = jnp.where(low, center, jnp.where(beside, roll(corner, shift, 1), 0.0))

        outer(67, top, 64)
        outer(68, roll(top, 64, 1), 0)
        outer(69, mid, 56)
        outer(0, roll(mid, 64, 1), 80)
        outer(1, end, 8)
        outer(2, roll(end, 64, 1), 72)
        for block in range(4):
            side = added(q, own_cols, got_cols, block)
            for t in range(8):
                for o in range(2):
                    row = 3 + 16 * block + 2 * t + o
                    near = roll(side, 64 * (1 - o) - 8 * t, 1)
                    dst[row] = dst[row] + jnp.where(beside, near, 0.0)

    arrive(ROWS_X, "x", r1_src, r1_dst)
    lax.fori_loop(0, N, make_row_masks, 0)
    choose_rows(rows_t, rows_s)
    r2_src, r2_dst = (lambda p: rows_s.at[p]), (lambda p: rows_g.at[p])
    start(ROWS_Y, "y", r2_src, r2_dst)
    arrive(COLS_Y, "y", c1_src, c1_dst)
    lax.fori_loop(0, N, make_col_masks, 0)
    choose_cols(cols_t, cols_s)
    c2_src, c2_dst = (lambda p: cols_s.at[p]), (lambda p: cols_g.at[p])
    start(COLS_X, "x", c2_src, c2_dst)
    arrive(ROWS_Y, "y", r2_src, r2_dst)
    arrive(COLS_X, "x", c2_src, c2_dst)
    finish_halo(rows_s, rows_g, cols_s, cols_g, xpad)

    def filtered(src, flip, r):
        total = None
        for b in range(7):
            part = None
            for a in range(7):
                tap = (6 - a) * 7 + 6 - b if flip else a * 7 + b
                term = wb[tap][None] * src[pl.ds(8 * r + a, 8)]
                part = term if part is None else part + term
            part = roll(part, 3 - b, 2)
            total = part if total is None else total + part
        return [jnp.where(low, total[2 * u], roll(total[2 * u + 1], 64, 1)) for u in range(4)]

    c_src, c_dst = (lambda p: conv_r.at[:, lanes(p, 512)]), (lambda p: convs.at[rows16(p), :])
    a_src, a_dst = (lambda p: means.at[:, lanes(p, 512)]), (lambda p: mean_all.at[p])

    def forward(j, carry):
        r = lax.rem(z + 1 + j, N)
        tiles = filtered(xpad, False, r)
        for u in range(4):
            mean = jnp.sum(tiles[u], 0, keepdims=True) * (1.0 / 16)
            conv_r[:, lanes(4 * r + u)] = (tiles[u] - mean).astype(BF16)
            means[:, lanes(4 * r + u)] = mean

        @pl.when(j < N - 1)
        def _():
            copy(CONV, "z", c_src(r), c_dst(z), r, z).start()
            copy(MEANS, "z", a_src(r), a_dst(z), r, z).start()

        return carry

    lax.fori_loop(0, N, forward, 0)
    sent.append((CONV, "z", c_src, c_dst))
    sent.append((MEANS, "z", a_src, a_dst))
    convs[rows16(z), :] = conv_r[:, lanes(z, 512)]
    mean_all[z] = means[:, lanes(z, 512)]
    arrive(CONV, "z", c_src, c_dst)
    arrive(MEANS, "z", a_src, a_dst)

    local = mean_all[...]
    mean = jnp.sum(local, 0) * (1.0 / N)
    centred = (convs[...].astype(F32).reshape(N, 16, 512) + (local - mean[None])).reshape(128, 512)
    rstd = lax.rsqrt(jnp.sum(centred * centred, 0, keepdims=True) * (1.0 / 128) + EPS)
    normed[...] = centred * rstd
    diagonal = lax.broadcasted_iota(jnp.int32, (128, 128), 0) == lax.broadcasted_iota(
        jnp.int32, (128, 128), 1
    )
    gain_col = jnp.sum(jnp.where(diagonal, jnp.broadcast_to(gain[...], (128, 128)), 0.0), 1, keepdims=True)
    feats[...] = (normed[...] * gain_col).astype(BF16)
    arrive(WEIGHTS, "z", w_src, w_dst)
    arrive(MASKED, "z", m_src, m_dst)

    def hidden(g, carry):
        wi = weights[pl.ds(2 * g, 2), 0:64, :].reshape(128, 128)
        wo = weights[pl.ds(2 * g, 2), 64:128, :].reshape(128, 128)
        pre = dot(wi, feats[...], ((1,), (0,)))
        square = pre * pre
        bend = jnp.tanh(0.7978845608 * pre * (1.0 + 0.044715 * square))
        half = 0.5 + 0.5 * bend
        act_h2[lanes(g), :] = (pre * half).astype(BF16)
        slope = half + (0.5 * 0.7978845608) * pre * (1.0 - bend * bend) * (
            1.0 + (3.0 * 0.044715) * square
        )
        d_act = dot(wo, dz[...], ((1,), (0,)))
        dpre_h[lanes(g), :] = (d_act * slope).astype(BF16)
        return carry

    lax.fori_loop(0, 4, hidden, 0)
    wi_all = weights[:, 0:64, :].reshape(512, 128)
    wo_all = weights[:, 64:128, :].reshape(512, 128)
    d_feat = dot(wi_all, dpre_h[...], ((0,), (0,)))
    per_gain = d_feat * normed[...]
    d_norm = d_feat * gain_col
    first = jnp.sum(d_norm, 0, keepdims=True) * (1.0 / 128)
    second = jnp.sum(per_gain * gain_col, 0, keepdims=True) * (1.0 / 128)
    dconv_s[...] = (rstd * (d_norm - first - normed[...] * second)).astype(BF16)
    d_src, d_dst = (lambda p: dconv_s.at[rows16(p), :]), (lambda p: dconv.at[:, lanes(p, 512)])
    start(DCONV, "z", d_src, d_dst)
    dconv[:, lanes(z, 512)] = dconv_s[rows16(z), :]

    g_s[:, 0:64, :] = dot(dpre_h[...], feats[...], ((1,), (1,))).astype(BF16).reshape(N, 64, 128)
    g_s[:, 64:128, :] = dot(act_h2[...], dz[...], ((1,), (1,))).astype(BF16).reshape(N, 64, 128)
    gx_src, gx_dst = (lambda p: g_s.at[:, rows16(p), :]), (lambda p: g_x.at[p])
    start(G_X, "x", gx_src, gx_dst)
    g_x[q] = g_s[:, rows16(q), :]
    branch_s[...] = dot(wo_all, act_h2[...], ((0,), (0,))).astype(BF16)
    branch[:, lanes(z, 512)] = branch_s[rows16(z), :]
    folded = per_gain[:, 0:128] + per_gain[:, 128:256] + per_gain[:, 256:384] + per_gain[:, 384:512]
    gain_s[...] = folded.reshape(N, 16, 128)
    gains[z] = gain_s[z]

    arrive(DCONV, "z", d_src, d_dst)
    build_cols(dconv, d_cols)
    e1_src, e1_dst = (lambda p: d_cols), (lambda p: d_cols_t.at[p])
    start(D_COLS_Y, "y", e1_src, e1_dst)
    build_rows(dconv, d_rows)
    f1_src, f1_dst = (lambda p: d_rows), (lambda p: d_rows_t.at[p])
    start(D_ROWS_X, "x", f1_src, f1_dst)
    d_cols_t[y] = d_cols[...]
    d_rows_t[q] = d_rows[...]

    arrive(G_X, "x", gx_src, gx_dst)
    g_xs[...] = jnp.sum(g_x[...].astype(F32), 0)
    gz_src, gz_dst = (lambda p: g_xs.at[p]), (lambda p: g_z.at[p])
    start(G_Z, "z", gz_src, gz_dst)
    g_z[z] = g_xs[z]
    n_src, n_dst = (lambda p: gain_s.at[p]), (lambda p: gains.at[p])
    start(GAIN, "z", n_src, n_dst)
    b_src, b_dst = (lambda p: branch_s.at[rows16(p), :]), (lambda p: branch.at[:, lanes(p, 512)])
    start(BRANCH, "z", b_src, b_dst)
    spread(dconv, dpad)

    def filter_grad(small, columns):
        for b in columns:

            def taps(r, carry, b=b):
                moved = roll(dpad[pl.ds(3 + 8 * r, 8)], b - 3, 2)
                return tuple(
                    carry[a] + jnp.sum(moved * xpad[pl.ds(8 * r + a, 8)], 0) for a in range(7)
                )

            column = lax.fori_loop(0, 8, taps, tuple(jnp.zeros((16, 128), F32) for _ in range(7)))
            for a in range(7):
                small = jnp.where(lane == a * 7 + b, jnp.sum(column[a], 1, keepdims=True), small)
        return small

    small = filter_grad(jnp.zeros((16, 128), F32), range(0, 4))
    arrive(D_ROWS_X, "x", f1_src, f1_dst)
    choose_rows(d_rows_t, d_rows_s)
    f2_src, f2_dst = (lambda p: d_rows_s.at[p]), (lambda p: d_rows_g.at[p])
    start(D_ROWS_Y, "y", f2_src, f2_dst)
    small = filter_grad(small, range(4, 6))
    arrive(D_COLS_Y, "y", e1_src, e1_dst)
    choose_cols(d_cols_t, d_cols_s)
    e2_src, e2_dst = (lambda p: d_cols_s.at[p]), (lambda p: d_cols_g.at[p])
    start(D_COLS_X, "x", e2_src, e2_dst)
    small = filter_grad(small, range(6, 7))
    arrive(GAIN, "z", n_src, n_dst)
    small = jnp.where(lane == 49, jnp.sum(jnp.sum(gains[...], 0), 1, keepdims=True), small)
    s_y[y] = small
    sy_src, sy_dst = (lambda p: s_y.at[y]), (lambda p: s_y.at[p])
    start(S_Y, "y", sy_src, sy_dst)

    arrive(G_Z, "z", gz_src, gz_dst)
    g_y[y] = jnp.sum(g_z[...], 0)
    gy_src, gy_dst = (lambda p: g_y.at[y]), (lambda p: g_y.at[p])
    start(G_Y, "y", gy_src, gy_dst)

    arrive(BRANCH, "z", b_src, b_dst)

    def write_out(t, carry):
        at = lanes(t, 512)
        kept = mask[:, at].astype(F32)
        out[:, at] = (act[:, at].astype(F32) + kept * branch[:, at].astype(F32)).astype(BF16)
        return carry

    lax.fori_loop(0, 8, write_out, 0)
    stores[0].start()

    arrive(D_ROWS_Y, "y", f2_src, f2_dst)
    arrive(D_COLS_X, "x", e2_src, e2_dst)
    finish_halo(d_rows_s, d_rows_g, d_cols_s, d_cols_g, dpad)

    arrive(S_Y, "y", sy_src, sy_dst)
    s_x[q] = jnp.sum(s_y[...], 0)
    sx_src, sx_dst = (lambda p: s_x.at[q]), (lambda p: s_x.at[p])
    start(S_X, "x", sx_src, sx_dst)
    arrive(G_Y, "y", gy_src, gy_dst)
    g_all[q] = jnp.sum(g_y[...], 0)
    ga_src, ga_dst = (lambda p: g_all.at[q]), (lambda p: g_all.at[p])
    start(G_ALL, "x", ga_src, ga_dst)

    def backward(r, carry):
        tiles = filtered(dpad, True, r)
        for u in range(4):
            at = lanes(4 * r + u)
            igrad[:, at] = (cot[:, at].astype(F32) + tiles[u]).astype(BF16)
        return carry

    lax.fori_loop(0, N, backward, 0)
    stores[1].start()

    arrive(S_X, "x", sx_src, sx_dst)
    small = jnp.sum(s_x[...], 0)
    kgrad_out[...] = small[:, 0:49]
    square16 = lax.broadcasted_iota(jnp.int32, (16, 16), 0) == lax.broadcasted_iota(
        jnp.int32, (16, 16), 1
    )
    gain_out[...] = jnp.sum(
        jnp.where(square16, jnp.broadcast_to(small[:, 49:50], (16, 16)), 0.0), 0, keepdims=True
    )
    stores[2].start()
    stores[3].start()
    arrive(G_ALL, "x", ga_src, ga_dst)
    both = g_all[...].reshape(128, 128)
    w_in_out[...] = both[0:64]
    w_out_out[...] = both[64:128]
    stores[4].start()
    stores[5].start()
    for stage, group, src, dst in sent:
        me = mine[group]
        peers(group, lambda p: copy(stage, group, src(p), dst(me), p, me).wait_send())
    for store in stores:
        store.wait()


def finish_body(*refs):
    count = len(refs) // 2
    sems = refs[-1]
    copies = [
        pltpu.make_async_copy(refs[i], refs[count + i], sems.at[i]) for i in range(count)
    ]
    for move in copies:
        move.start()
    for move in copies:
        move.wait()


def body(activations, cotangent, kernel, gain, w_in, w_out, neighbours, land_mask):
    anywhere = pl.BlockSpec(memory_space=pl.ANY)
    scratch = [
        ((16, 4096), BF16),
        ((16, 4096), BF16),
        ((16, 49), F32),
        ((1, 128), F32),
        ((64, 128), BF16),
        ((64, 128), BF16),
        ((1, 8), jnp.int32),
        ((1, 4096), jnp.int32),
        ((16, 4096), BF16),
        ((16, 4096), BF16),
        ((16, 49), F32),
        ((1, 16), F32),
        ((64, 128), F32),
        ((64, 128), F32),
        ((70, 16, 128), F32),
        ((70, 16, 128), F32),
        ((49, 16, 128), F32),
        ((64, 128), BF16),
        ((80, 128), BF16),
        ((48, 128), BF16),
        ((64, 128), BF16),
        ((N, 64, 128), BF16),
        ((N, 80, 128), BF16),
        ((N, 48, 128), BF16),
        ((N, 64, 128), BF16),
        ((N, N, 8, 128), F32),
        ((N, N, 8, 128), F32),
        ((N, 48, 128), BF16),
        ((N, 80, 128), BF16),
        ((N, 48, 128), BF16),
        ((N, 80, 128), BF16),
        ((N, 48, 128), BF16),
        ((N, 80, 128), BF16),
        ((N, 48, 128), BF16),
        ((N, 80, 128), BF16),
        ((N, 128, 128), BF16),
        ((16, 4096), BF16),
        ((16, 4096), BF16),
        ((1, 4096), F32),
        ((128, 512), BF16),
        ((N, 1, 512), F32),
        ((128, 512), BF16),
        ((128, 512), F32),
        ((128, 512), BF16),
        ((512, 512), BF16),
        ((512, 512), BF16),
        ((128, 512), BF16),
        ((16, 4096), BF16),
        ((128, 512), BF16),
        ((16, 4096), BF16),
        ((N, 16, 128), F32),
        ((N, 16, 128), F32),
        ((N, 128, 128), BF16),
        ((N, N, 16, 128), BF16),
        ((N, 16, 128), F32),
        ((N, 16, 128), F32),
        ((N, 16, 128), F32),
        ((N, 16, 128), F32),
        ((N, 16, 128), F32),
        ((N, 16, 128), F32),
    ]
    shapes = [
        jax.ShapeDtypeStruct((16, 4096), BF16),
        jax.ShapeDtypeStruct((16, 4096), BF16),
        jax.ShapeDtypeStruct((16, 49), F32),
        jax.ShapeDtypeStruct((1, 16), F32),
        jax.ShapeDtypeStruct((64, 128), F32),
        jax.ShapeDtypeStruct((64, 128), F32),
    ]
    results = pl.pallas_call(
        kernel_body,
        out_shape=shapes,
        in_specs=[anywhere] * 8,
        out_specs=[anywhere] * 6,
        scratch_shapes=[pltpu.VMEM(shape, kind) for shape, kind in scratch]
        + [
            pltpu.SemaphoreType.DMA((21, N)),
            pltpu.SemaphoreType.DMA((21, N)),
            pltpu.SemaphoreType.DMA((8,)),
            pltpu.SemaphoreType.DMA((6,)),
        ],
        compiler_params=pltpu.CompilerParams(
            collective_id=0, has_side_effects=True, vmem_limit_bytes=VMEM_LIMIT
        ),
        cost_estimate=pl.CostEstimate(flops=360000000, bytes_accessed=1000000, transcendentals=262144),
        name="block",
    )(
        activations[0], cotangent[0], kernel, gain.reshape(1, 128), w_in.T, w_out, neighbours, land_mask,
    )
    out, igrad, kgrad, ggrad, wigrad, wograd = pl.pallas_call(
        finish_body,
        out_shape=shapes,
        in_specs=[anywhere] * 6,
        out_specs=[anywhere] * 6,
        scratch_shapes=[pltpu.SemaphoreType.DMA((6,))],
        compiler_params=pltpu.CompilerParams(vmem_limit_bytes=VMEM_LIMIT),
        name="results",
    )(*results)
    return (out[None], igrad[None], kgrad, ggrad.reshape(16), wigrad.T, wograd)


def solution(mesh):
    placed = (
        P("tile", "chan", None),
        P("tile", "chan", None),
        P("chan", None),
        P(),
        P(None, "chan"),
        P("chan", None),
        P("tile", None),
        P("tile", None),
    )
    return jax.shard_map(
        body,
        mesh=mesh,
        in_specs=placed,
        out_specs=(
            P("tile", "chan", None),
            P("tile", "chan", None),
            P("chan", None),
            P("chan"),
            P(None, "chan"),
            P("chan", None),
        ),
        check_vma=False,
    )
```

```python
import jax
import jax.numpy as jnp
from jax import lax
from jax.experimental import pallas as pl
from jax.experimental.pallas import tpu as pltpu
from jax.sharding import PartitionSpec as P

EPS = 1e-06
N = 8
F32 = jnp.float32
BF16 = jnp.bfloat16
VMEM_LIMIT = 60 * 1024 * 1024

(
    ROWS_X, COLS_Y, ROWS_Y, COLS_X, D_ROWS_X, D_COLS_Y, D_ROWS_Y, D_COLS_X,
    WEIGHTS, MASKED, CONV, MEANS, DCONV, BRANCH, GAIN, G_X, G_Z, G_Y, G_ALL, S_Y, S_X,
) = range(21)


def dot(a, b, dims):
    return lax.dot_general(a, b, (dims, ((), ())), preferred_element_type=F32)


def lanes(t, width=128):
    return pl.ds(pl.multiple_of(t * width, width), width)


def rows16(p):
    return pl.ds(pl.multiple_of(p * 16, 16), 16)


def kernel_body(
    act_h, cot_h, ker_h, gain_h, w_in_h, w_out_h, nbr_h, mask_h,
    out_h, igrad_h, kgrad_h, ggrad_h, w_in_grad_h, w_out_grad_h,
    act, cot, ker, gain, w_in, w_out, nbr, mask,
    out, igrad, kgrad_out, gain_out, w_in_out, w_out_out,
    xpad, dpad, wb, rows, cols, d_rows, d_cols,
    rows_t, cols_t, d_rows_t, d_cols_t, row_masks, col_masks,
    rows_s, cols_s, d_rows_s, d_cols_s, rows_g, cols_g, d_rows_g, d_cols_g,
    outers, sides, fixes, conv_c, back_c, sums,
    weights, masked, conv_r, means, convs, mean_all, dz, normed, feats, act_h2, dpre_h,
    dconv_s, dconv, branch_s, branch, gain_s, gains, g_s, g_x, g_xs, g_z, g_y, g_all, s_y, s_x,
    ssem, rsem, lsem, osem,
):
    tile = lax.axis_index("tile")
    z = lax.axis_index("chan")
    y = tile // N
    q = lax.rem(tile, N)
    mine = {"y": y, "x": q, "z": z}

    def device(group, p):
        if group == "y":
            return (p * N + q, z)
        if group == "x":
            return (y * N + p, z)
        return (tile, p)

    def copy(stage, group, src, dst, to, slot):
        return pltpu.make_async_remote_copy(
            src_ref=src,
            dst_ref=dst,
            send_sem=ssem.at[stage, to],
            recv_sem=rsem.at[stage, slot],
            device_id=device(group, to),
            device_id_type=pl.DeviceIdType.MESH,
        )

    def peers(group, step):
        def one(j, carry):
            step(lax.rem(mine[group] + 4 + (1 - 2 * lax.rem(j, 2)) * ((j + 1) // 2), N))
            return carry

        lax.fori_loop(0, N - 1, one, 0)

    sent = []

    def start(stage, group, src, dst):
        me = mine[group]
        peers(group, lambda p: copy(stage, group, src(p), dst(me), p, me).start())
        sent.append((stage, group, src, dst))

    def arrive(stage, group, src, dst):
        peers(group, lambda p: copy(stage, group, src(p), dst(p), p, p).wait_recv())

    def settle():
        for stage, group, src, dst in sent:
            me = mine[group]
            peers(group, lambda p: copy(stage, group, src(p), dst(me), p, me).wait_send())
        sent.clear()

    lane = lax.broadcasted_iota(jnp.int32, (16, 128), 1)
    lane1 = lax.broadcasted_iota(jnp.int32, (1, 1, 128), 2)
    low = lane < 64
    rest = lane & 63
    edge = (rest < 3) | (rest >= 61)
    beside = ((lane >= 64) & (lane < 67)) | (lane >= 125)

    def window_in(index, members):
        found = index < 0
        for member in members:
            found = found | (index == member)
        return found

    def pair(ref, t):
        return ref[:, lanes(t)].astype(F32)

    def roll(x, shift, axis):
        shift = shift % 128
        return x if shift == 0 else pltpu.roll(x, shift, axis)

    inputs = [
        (act_h, act), (nbr_h, nbr), (cot_h, cot), (mask_h, mask),
        (w_in_h, w_in), (w_out_h, w_out), (ker_h, ker), (gain_h, gain),
    ]
    loads = [pltpu.make_async_copy(src, dst, lsem.at[i]) for i, (src, dst) in enumerate(inputs)]
    for load in loads:
        load.start()
    results = [
        (out, out_h), (igrad, igrad_h), (kgrad_out, kgrad_h), (gain_out, ggrad_h),
        (w_in_out, w_in_grad_h), (w_out_out, w_out_grad_h),
    ]
    stores = [pltpu.make_async_copy(src, dst, osem.at[i]) for i, (src, dst) in enumerate(results)]

    barrier = pltpu.get_barrier_semaphore()
    for group in ("y", "x", "z"):
        peers(
            group,
            lambda p, group=group: pl.semaphore_signal(
                barrier, inc=1, device_id=device(group, p), device_id_type=pl.DeviceIdType.MESH
            ),
        )

    def build_rows(src, dst):
        dst[0:16, :] = src[:, 0:128]
        dst[16:32, :] = jnp.where(low, pair(src, 1), pair(src, 30)).astype(BF16)
        dst[32:48, :] = src[:, 3968:4096]

    def build_cols(src, dst):
        for block in range(4):
            total = jnp.zeros((16, 128), F32)
            for t in range(8):
                total = total + roll(jnp.where(edge, pair(src, block * 8 + t), 0.0), 8 * t, 1)
            dst[16 * block : 16 * block + 16, :] = total.astype(BF16)

    loads[0].wait()
    build_cols(act, cols)
    build_rows(act, rows)
    loads[1].wait()
    eight = lax.broadcasted_iota(jnp.int32, (16, 8), 0) == lax.broadcasted_iota(jnp.int32, (16, 8), 1)
    listed = jnp.sum(
        jnp.where(eight, jnp.broadcast_to(nbr[...].astype(F32), (16, 8)), 0.0), 1, keepdims=True
    )
    listed = jnp.broadcast_to(listed, (16, 128)).astype(BF16)
    rows[48:64, :] = listed
    cols[64:80, :] = listed

    pl.semaphore_wait(barrier, 3 * (N - 1))
    c1_src, c1_dst = (lambda p: cols), (lambda p: cols_t.at[p])
    start(COLS_Y, "y", c1_src, c1_dst)
    r1_src, r1_dst = (lambda p: rows), (lambda p: rows_t.at[p])
    start(ROWS_X, "x", r1_src, r1_dst)
    cols_t[y] = cols[...]
    rows_t[q] = rows[...]

    for load in loads[2:]:
        load.wait()
    weights[z, 0:64, :] = w_in[...]
    weights[z, 64:128, :] = w_out[...]
    w_src, w_dst = (lambda p: weights.at[z]), (lambda p: weights.at[p])
    start(WEIGHTS, "z", w_src, w_dst)

    def mask_cot(t, carry):
        kept = mask[:, lanes(t, 512)].astype(F32)
        masked[:, lanes(t, 512)] = (cot[:, lanes(t, 512)].astype(F32) * kept).astype(BF16)
        return carry

    lax.fori_loop(0, 8, mask_cot, 0)
    m_src, m_dst = (lambda p: masked.at[:, lanes(p, 512)]), (lambda p: dz.at[rows16(p), :])
    start(MASKED, "z", m_src, m_dst)
    dz[rows16(z), :] = masked[:, lanes(z, 512)]

    for tap in range(49):
        wb[tap] = jnp.broadcast_to(ker[:, tap : tap + 1], (16, 128))

    def spread(src, dst):
        def some(block, carry):
            for u in range(8):
                both = pair(src, 8 * block + u)
                dst[3 + 16 * block + 2 * u] = jnp.where(low, both, 0.0)
                dst[4 + 16 * block + 2 * u] = jnp.where(low, roll(both, 64, 1), 0.0)
            return carry

        for row in (0, 1, 2, 67, 68, 69):
            dst[row] = jnp.zeros((16, 128), F32)
        lax.fori_loop(0, 4, some, 0)

    spread(act, xpad)

    def filtered(src, flip, r):
        total = None
        for b in range(7):
            part = None
            for a in range(7):
                tap = (6 - a) * 7 + 6 - b if flip else a * 7 + b
                term = wb[tap][None] * src[pl.ds(8 * r + a, 8)]
                part = term if part is None else part + term
            part = roll(part, 3 - b, 2)
            total = part if total is None else total + part
        return [jnp.where(low, total[2 * u], roll(total[2 * u + 1], 64, 1)) for u in range(4)]

    def centre(src, flip, dst):
        def some(r, carry):
            tiles = filtered(src, flip, r)
            for u in range(4):
                dst[:, lanes(4 * r + u)] = tiles[u]
            return carry

        lax.fori_loop(0, N, some, 0)

    centre(xpad, False, conv_c)

    index4 = lane1 // 4
    odd = (index4 & 1) == 1
    in_top = window_in(index4, (0, 15, 16, 31, 2, 17))
    in_bottom = window_in(index4, (28, 11, 14, 29, 30, 13))

    def listed_as(table, first, number):
        near = (table[:, first : first + 16, :].astype(F32) == number.astype(F32)).astype(F32)
        return [near[:, k : k + 1, :] for k in range(8)]

    def make_col_masks(d, carry):
        m = listed_as(cols_t, 64, y * N + d)
        col_masks[d, :, 0:1, :] = jnp.where(odd, m[4], m[3])
        col_masks[d, :, 1:2, :] = jnp.where(
            in_top, jnp.where(odd, m[2], m[0]), jnp.where(in_bottom, jnp.where(odd, m[7], m[5]), 0.0)
        )
        return carry

    def make_row_masks(d, carry):
        m = listed_as(rows_t, 48, d * N + q)
        row_masks[d, :, 0:1, :] = m[1]
        row_masks[d, :, 1:2, :] = jnp.where(lane1 < 64, m[1], m[6])
        row_masks[d, :, 2:3, :] = m[6]
        return carry

    def choose_rows(src, dst):
        def one(d, carry):
            for part in range(3):
                block = src[:, 16 * part : 16 * part + 16, :].astype(F32)
                total = jnp.sum(row_masks[d, :, part : part + 1, :] * block, 0)
                dst[d, 16 * part : 16 * part + 16, :] = total.astype(BF16)
            return carry

        lax.fori_loop(0, N, one, 0)

    def choose_cols(src, dst):
        def one(d, carry):
            for part in range(4):
                block = src[:, 16 * part : 16 * part + 16, :].astype(F32)
                total = jnp.sum(col_masks[d, :, 0:1, :] * block, 0)
                dst[d, 16 * part : 16 * part + 16, :] = total.astype(BF16)
            block = jnp.where(in_bottom, src[:, 48:64, :].astype(F32), src[:, 0:16, :].astype(F32))
            dst[d, 64:80, :] = jnp.sum(col_masks[d, :, 1:2, :] * block, 0).astype(BF16)
            return carry

        lax.fori_loop(0, N, one, 0)

    def added(me, own, got, i):
        total = own[me, 16 * i : 16 * i + 16, :].astype(F32)
        for j in range(1, N):
            total = total + got[lax.rem(me + j, N), 16 * i : 16 * i + 16, :].astype(F32)
        return total

    block8, in8 = lane1 // 8, lane1 & 7
    place = jnp.where(in8 < 4, (block8 + 8) & 15, (block8 + 1) & 15)
    half, step = jnp.where(place < 8, 1, 0), place & 7

    def gather_halo(own_rows, got_rows, own_cols, got_cols):
        top, mid, end = [added(y, own_rows, got_rows, i) for i in range(3)]
        corner = added(q, own_cols, got_cols, 4)
        centres = (roll(mid, 64, 1), end, roll(end, 64, 1), top, roll(top, 64, 1), mid)
        for i, shift in enumerate((80, 8, 72, 64, 0, 56)):
            outers[i] = jnp.where(low, centres[i], jnp.where(beside, roll(corner, shift, 1), 0.0))
        sides[0] = jnp.zeros((16, 128), F32)
        sides[5] = jnp.zeros((16, 128), F32)
        for block in range(4):
            sides[1 + block] = added(q, own_cols, got_cols, block)

    def fill_pad(dst):
        for i, row in enumerate((0, 1, 2, 67, 68, 69)):
            dst[row] = outers[i]
        for block in range(4):
            side = sides[1 + block]
            for t in range(8):
                for o in range(2):
                    row = 3 + 16 * block + 2 * t + o
                    near = roll(side, 64 * (1 - o) - 8 * t, 1)
                    dst[row] = dst[row] + jnp.where(beside, near, 0.0)

    def fix_rows(flip, dst):
        def fixed(pieces):
            total = None
            for b in range(7):
                part = None
                for a, i in pieces:
                    tap = (6 - a) * 7 + 6 - b if flip else a * 7 + b
                    term = wb[tap] * outers[i]
                    part = term if part is None else part + term
                part = roll(part, 3 - b, 1)
                total = part if total is None else total + part
            return total

        tops = [fixed([(a, i + a) for a in range(3 - i)]) for i in range(3)]
        ends = [fixed([(6 - i + m, 3 + m) for m in range(i + 1)]) for i in range(3)]
        zero = jnp.zeros((16, 128), F32)
        for t, lower, upper in (
            (0, tops[0], tops[1]), (1, tops[2], zero), (30, zero, ends[0]), (31, ends[1], ends[2]),
        ):
            at = slice(128 * t, 128 * t + 128)
            dst[:, at] = dst[:, at] + jnp.where(low, lower, roll(upper, 64, 1))

    def fix_cols(flip):
        parts = [None] * 7
        for a in range(7):
            by = a - 3
            moved = sides[1:5]
            if by:
                moved = jnp.zeros((4, 16, 128), F32)
                for o in range(2):
                    up = (o + by) // 2
                    other = (o + by) - 2 * up
                    for over in (-1, 0, 1):
                        if over * up < 0 or (over and not up):
                            continue
                        fits = (half == o) & (step + up >= 8 * over) & (step + up < 8 * over + 8)
                        from_ = roll(sides[1 + over : 5 + over], -8 * (up - 8 * over + 8 * (o - other)), 2)
                        moved = jnp.where(fits, from_, moved)
            for b in (0, 1, 2, 4, 5, 6):
                tap = (6 - a) * 7 + 6 - b if flip else a * 7 + b
                term = wb[tap][None] * moved
                parts[b] = term if parts[b] is None else parts[b] + term
        total = jnp.zeros((4, 16, 128), F32)
        for b in (0, 1, 2, 4, 5, 6):
            lands = in8 < 3 - b if b < 3 else in8 > 10 - b
            total = total + jnp.where(lands, roll(parts[b], 3 - b, 2), 0.0)
        fixes[...] = total

    arrive(ROWS_X, "x", r1_src, r1_dst)
    lax.fori_loop(0, N, make_row_masks, 0)
    choose_rows(rows_t, rows_s)
    r2_src, r2_dst = (lambda p: rows_s.at[p]), (lambda p: rows_g.at[p])
    start(ROWS_Y, "y", r2_src, r2_dst)
    arrive(COLS_Y, "y", c1_src, c1_dst)
    lax.fori_loop(0, N, make_col_masks, 0)
    choose_cols(cols_t, cols_s)
    c2_src, c2_dst = (lambda p: cols_s.at[p]), (lambda p: cols_g.at[p])
    start(COLS_X, "x", c2_src, c2_dst)
    arrive(ROWS_Y, "y", r2_src, r2_dst)
    arrive(COLS_X, "x", c2_src, c2_dst)
    gather_halo(rows_s, rows_g, cols_s, cols_g)
    fix_rows(False, conv_c)
    fix_cols(False)

    c_src, c_dst = (lambda p: conv_r.at[:, lanes(p, 512)]), (lambda p: convs.at[rows16(p), :])
    a_src, a_dst = (lambda p: means.at[:, lanes(p, 512)]), (lambda p: mean_all.at[p])

    def forward(block, carry):
        for t in range(8):
            at = lanes(8 * block + t)
            whole = conv_c[:, at] + jnp.where(edge, roll(fixes[block], 64 - 8 * t, 1), 0.0)
            mean = jnp.sum(whole, 0, keepdims=True) * (1.0 / 16)
            conv_r[:, at] = (whole - mean).astype(BF16)
            means[:, at] = mean
        return carry

    lax.fori_loop(0, 4, forward, 0)
    start(CONV, "z", c_src, c_dst)
    start(MEANS, "z", a_src, a_dst)
    convs[rows16(z), :] = conv_r[:, lanes(z, 512)]
    mean_all[z] = means[:, lanes(z, 512)]
    fill_pad(xpad)
    settle()
    arrive(CONV, "z", c_src, c_dst)
    arrive(MEANS, "z", a_src, a_dst)

    local = mean_all[...]
    mean = jnp.sum(local, 0) * (1.0 / N)
    centred = (convs[...].astype(F32).reshape(N, 16, 512) + (local - mean[None])).reshape(128, 512)
    rstd = lax.rsqrt(jnp.sum(centred * centred, 0, keepdims=True) * (1.0 / 128) + EPS)
    normed[...] = centred * rstd
    diagonal = lax.broadcasted_iota(jnp.int32, (128, 128), 0) == lax.broadcasted_iota(
        jnp.int32, (128, 128), 1
    )
    gain_col = jnp.sum(jnp.where(diagonal, jnp.broadcast_to(gain[...], (128, 128)), 0.0), 1, keepdims=True)
    feats[...] = (normed[...] * gain_col).astype(BF16)
    arrive(WEIGHTS, "z", w_src, w_dst)
    arrive(MASKED, "z", m_src, m_dst)

    def hidden(g, carry):
        wi = weights[pl.ds(2 * g, 2), 0:64, :].reshape(128, 128)
        wo = weights[pl.ds(2 * g, 2), 64:128, :].reshape(128, 128)
        pre = dot(wi, feats[...], ((1,), (0,)))
        square = pre * pre
        bend = jnp.tanh(0.7978845608 * pre * (1.0 + 0.044715 * square))
        half = 0.5 + 0.5 * bend
        act_h2[lanes(g), :] = (pre * half).astype(BF16)
        slope = half + (0.5 * 0.7978845608) * pre * (1.0 - bend * bend) * (
            1.0 + (3.0 * 0.044715) * square
        )
        d_act = dot(wo, dz[...], ((1,), (0,)))
        dpre_h[lanes(g), :] = (d_act * slope).astype(BF16)
        return carry

    lax.fori_loop(0, 4, hidden, 0)
    wi_all = weights[:, 0:64, :].reshape(512, 128)
    wo_all = weights[:, 64:128, :].reshape(512, 128)
    g_s[:, 0:64, :] = dot(dpre_h[...], feats[...], ((1,), (1,))).astype(BF16).reshape(N, 64, 128)
    g_s[:, 64:128, :] = dot(act_h2[...], dz[...], ((1,), (1,))).astype(BF16).reshape(N, 64, 128)
    gx_src, gx_dst = (lambda p: g_s.at[:, rows16(p), :]), (lambda p: g_x.at[p])
    start(G_X, "x", gx_src, gx_dst)
    g_x[q] = g_s[:, rows16(q), :]

    d_feat = dot(wi_all, dpre_h[...], ((0,), (0,)))
    per_gain = d_feat * normed[...]
    d_norm = d_feat * gain_col
    first = jnp.sum(d_norm, 0, keepdims=True) * (1.0 / 128)
    second = jnp.sum(per_gain * gain_col, 0, keepdims=True) * (1.0 / 128)
    dconv_s[...] = (rstd * (d_norm - first - normed[...] * second)).astype(BF16)
    d_src, d_dst = (lambda p: dconv_s.at[rows16(p), :]), (lambda p: dconv.at[:, lanes(p, 512)])
    start(DCONV, "z", d_src, d_dst)
    dconv[:, lanes(z, 512)] = dconv_s[rows16(z), :]
    gain_sum = jnp.sum(per_gain, 1, keepdims=True)
    gain_s[...] = jnp.sum(jnp.where(diagonal, gain_sum, 0.0), 0, keepdims=True)
    n_src, n_dst = (lambda p: gain_s), (lambda p: gains.at[p])
    start(GAIN, "z", n_src, n_dst)
    gains[z] = gain_s[...]

    branch_s[...] = dot(wo_all, act_h2[...], ((0,), (0,))).astype(BF16)
    branch[:, lanes(z, 512)] = branch_s[rows16(z), :]
    arrive(DCONV, "z", d_src, d_dst)
    build_cols(dconv, d_cols)
    e1_src, e1_dst = (lambda p: d_cols), (lambda p: d_cols_t.at[p])
    start(D_COLS_Y, "y", e1_src, e1_dst)
    build_rows(dconv, d_rows)
    f1_src, f1_dst = (lambda p: d_rows), (lambda p: d_rows_t.at[p])
    start(D_ROWS_X, "x", f1_src, f1_dst)
    d_cols_t[y] = d_cols[...]
    d_rows_t[q] = d_rows[...]

    arrive(G_X, "x", gx_src, gx_dst)
    g_xs[...] = jnp.sum(g_x[...].astype(F32), 0).astype(BF16)
    gz_src, gz_dst = (lambda p: g_xs.at[p]), (lambda p: g_z.at[p])
    start(G_Z, "z", gz_src, gz_dst)
    g_z[z] = g_xs[z]
    spread(dconv, dpad)

    def taps(r, carry):
        for b in range(7):
            moved = roll(dpad[pl.ds(3 + 8 * r, 8)], b - 3, 2)
            for a in range(7):
                sums[a * 7 + b] += jnp.sum(moved * xpad[pl.ds(8 * r + a, 8)], 0)
        return carry

    sums[...] = jnp.zeros((49, 16, 128), F32)
    lax.fori_loop(0, 8, taps, 0)
    small = jnp.zeros((16, 128), F32)
    for tap in range(49):
        small = jnp.where(lane == tap, jnp.sum(sums[tap], 1, keepdims=True), small)
    arrive(GAIN, "z", n_src, n_dst)
    sub = lax.broadcasted_iota(jnp.int32, (16, 128), 0)
    gain_mine = jnp.where(lane == sub + 16 * z, jnp.broadcast_to(jnp.sum(gains[...], 0), (16, 128)), 0.0)
    small = jnp.where(lane == 49, jnp.sum(gain_mine, 1, keepdims=True), small)
    s_y[y] = small
    sy_src, sy_dst = (lambda p: s_y.at[y]), (lambda p: s_y.at[p])
    start(S_Y, "y", sy_src, sy_dst)

    arrive(D_ROWS_X, "x", f1_src, f1_dst)
    choose_rows(d_rows_t, d_rows_s)
    f2_src, f2_dst = (lambda p: d_rows_s.at[p]), (lambda p: d_rows_g.at[p])
    start(D_ROWS_Y, "y", f2_src, f2_dst)
    arrive(G_Z, "z", gz_src, gz_dst)
    g_y[y] = jnp.sum(g_z[...].astype(F32), 0)
    gy_src, gy_dst = (lambda p: g_y.at[y]), (lambda p: g_y.at[p])
    start(G_Y, "y", gy_src, gy_dst)
    arrive(D_COLS_Y, "y", e1_src, e1_dst)
    choose_cols(d_cols_t, d_cols_s)
    e2_src, e2_dst = (lambda p: d_cols_s.at[p]), (lambda p: d_cols_g.at[p])
    start(D_COLS_X, "x", e2_src, e2_dst)
    b_src, b_dst = (lambda p: branch_s.at[rows16(p), :]), (lambda p: branch.at[:, lanes(p, 512)])
    start(BRANCH, "z", b_src, b_dst)
    centre(dpad, True, back_c)

    arrive(S_Y, "y", sy_src, sy_dst)
    s_x[q] = jnp.sum(s_y[...], 0)
    sx_src, sx_dst = (lambda p: s_x.at[q]), (lambda p: s_x.at[p])
    start(S_X, "x", sx_src, sx_dst)
    arrive(G_Y, "y", gy_src, gy_dst)
    g_all[q] = jnp.sum(g_y[...], 0)
    ga_src, ga_dst = (lambda p: g_all.at[q]), (lambda p: g_all.at[p])
    start(G_ALL, "x", ga_src, ga_dst)

    arrive(D_ROWS_Y, "y", f2_src, f2_dst)
    arrive(D_COLS_X, "x", e2_src, e2_dst)
    gather_halo(d_rows_s, d_rows_g, d_cols_s, d_cols_g)
    fix_rows(True, back_c)
    fix_cols(True)

    def backward(block, carry):
        for t in range(8):
            at = lanes(8 * block + t)
            whole = back_c[:, at] + jnp.where(edge, roll(fixes[block], 64 - 8 * t, 1), 0.0)
            igrad[:, at] = (cot[:, at].astype(F32) + whole).astype(BF16)
        return carry

    lax.fori_loop(0, 4, backward, 0)
    stores[1].start()

    arrive(BRANCH, "z", b_src, b_dst)

    def write_out(t, carry):
        at = lanes(t, 512)
        kept = mask[:, at].astype(F32)
        out[:, at] = (act[:, at].astype(F32) + kept * branch[:, at].astype(F32)).astype(BF16)
        return carry

    lax.fori_loop(0, 8, write_out, 0)
    stores[0].start()

    settle()
    arrive(S_X, "x", sx_src, sx_dst)
    small = jnp.sum(s_x[...], 0)
    kgrad_out[...] = small[:, 0:49]
    square16 = lax.broadcasted_iota(jnp.int32, (16, 16), 0) == lax.broadcasted_iota(
        jnp.int32, (16, 16), 1
    )
    gain_out[...] = jnp.sum(
        jnp.where(square16, jnp.broadcast_to(small[:, 49:50], (16, 16)), 0.0), 0, keepdims=True
    )
    stores[2].start()
    stores[3].start()
    arrive(G_ALL, "x", ga_src, ga_dst)
    both = g_all[...].reshape(128, 128)
    w_in_out[...] = both[0:64]
    w_out_out[...] = both[64:128]
    stores[4].start()
    stores[5].start()
    settle()
    for store in stores:
        store.wait()


def finish_body(*refs):
    count = (len(refs) - 2) // 3
    arrays, results, held = refs[:count], refs[count : 2 * count], refs[2 * count : 3 * count]
    came, went = refs[-2:]
    loads = [pltpu.make_async_copy(arrays[i], held[i], came.at[i]) for i in range(count)]
    stores = [pltpu.make_async_copy(held[i], results[i], went.at[i]) for i in range(count)]
    for load in loads:
        load.start()
    for load, store in zip(loads, stores):
        load.wait()
        store.start()
    for store in stores:
        store.wait()


def body(activations, cotangent, kernel, gain, w_in, w_out, neighbours, land_mask):
    anywhere = pl.BlockSpec(memory_space=pl.ANY)
    scratch = [
        ((16, 4096), BF16),
        ((16, 4096), BF16),
        ((16, 49), F32),
        ((1, 128), F32),
        ((64, 128), BF16),
        ((64, 128), BF16),
        ((1, 8), jnp.int32),
        ((1, 4096), jnp.int32),
        ((16, 4096), BF16),
        ((16, 4096), BF16),
        ((16, 49), F32),
        ((1, 16), F32),
        ((64, 128), F32),
        ((64, 128), F32),
        ((70, 16, 128), F32),
        ((70, 16, 128), F32),
        ((49, 16, 128), F32),
        ((64, 128), BF16),
        ((80, 128), BF16),
        ((48, 128), BF16),
        ((64, 128), BF16),
        ((N, 64, 128), BF16),
        ((N, 80, 128), BF16),
        ((N, 48, 128), BF16),
        ((N, 64, 128), BF16),
        ((N, N, 8, 128), F32),
        ((N, N, 8, 128), F32),
        ((N, 48, 128), BF16),
        ((N, 80, 128), BF16),
        ((N, 48, 128), BF16),
        ((N, 80, 128), BF16),
        ((N, 48, 128), BF16),
        ((N, 80, 128), BF16),
        ((N, 48, 128), BF16),
        ((N, 80, 128), BF16),
        ((6, 16, 128), F32),
        ((6, 16, 128), F32),
        ((4, 16, 128), F32),
        ((16, 4096), F32),
        ((16, 4096), F32),
        ((49, 16, 128), F32),
        ((N, 128, 128), BF16),
        ((16, 4096), BF16),
        ((16, 4096), BF16),
        ((1, 4096), F32),
        ((128, 512), BF16),
        ((N, 1, 512), F32),
        ((128, 512), BF16),
        ((128, 512), F32),
        ((128, 512), BF16),
        ((512, 512), BF16),
        ((512, 512), BF16),
        ((128, 512), BF16),
        ((16, 4096), BF16),
        ((128, 512), BF16),
        ((16, 4096), BF16),
        ((1, 128), F32),
        ((N, 1, 128), F32),
        ((N, 128, 128), BF16),
        ((N, N, 16, 128), BF16),
        ((N, 16, 128), BF16),
        ((N, 16, 128), BF16),
        ((N, 16, 128), F32),
        ((N, 16, 128), F32),
        ((N, 16, 128), F32),
        ((N, 16, 128), F32),
    ]
    shapes = [
        jax.ShapeDtypeStruct((16, 4096), BF16),
        jax.ShapeDtypeStruct((16, 4096), BF16),
        jax.ShapeDtypeStruct((16, 49), F32),
        jax.ShapeDtypeStruct((1, 16), F32),
        jax.ShapeDtypeStruct((64, 128), F32),
        jax.ShapeDtypeStruct((64, 128), F32),
    ]
    results = pl.pallas_call(
        kernel_body,
        out_shape=shapes,
        in_specs=[anywhere] * 8,
        out_specs=[anywhere] * 6,
        scratch_shapes=[pltpu.VMEM(shape, kind) for shape, kind in scratch]
        + [
            pltpu.SemaphoreType.DMA((21, N)),
            pltpu.SemaphoreType.DMA((21, N)),
            pltpu.SemaphoreType.DMA((8,)),
            pltpu.SemaphoreType.DMA((6,)),
        ],
        compiler_params=pltpu.CompilerParams(
            collective_id=0, has_side_effects=True, vmem_limit_bytes=VMEM_LIMIT
        ),
        cost_estimate=pl.CostEstimate(flops=360000000, bytes_accessed=1000000, transcendentals=262144),
        name="block",
    )(
        activations[0], cotangent[0], kernel, gain.reshape(1, 128), w_in.T, w_out, neighbours, land_mask,
    )
    out, igrad, kgrad, ggrad, wigrad, wograd = pl.pallas_call(
        finish_body,
        out_shape=shapes,
        in_specs=[anywhere] * 6,
        out_specs=[anywhere] * 6,
        scratch_shapes=[pltpu.VMEM(result.shape, result.dtype) for result in shapes]
        + [pltpu.SemaphoreType.DMA((6,)), pltpu.SemaphoreType.DMA((6,))],
        compiler_params=pltpu.CompilerParams(vmem_limit_bytes=VMEM_LIMIT),
        name="results",
    )(*results)
    return (out[None], igrad[None], kgrad, ggrad.reshape(16), wigrad.T, wograd)


def solution(mesh):
    placed = (
        P("tile", "chan", None),
        P("tile", "chan", None),
        P("chan", None),
        P(),
        P(None, "chan"),
        P("chan", None),
        P("tile", None),
        P("tile", None),
    )
    return jax.shard_map(
        body,
        mesh=mesh,
        in_specs=placed,
        out_specs=(
            P("tile", "chan", None),
            P("tile", "chan", None),
            P("chan", None),
            P("chan"),
            P(None, "chan"),
            P("chan", None),
        ),
        check_vma=False,
    )
```

```python
import jax
import jax.numpy as jnp
from jax import lax
from jax.experimental import pallas as pl
from jax.experimental.pallas import tpu as pltpu
from jax.sharding import PartitionSpec as P

EPS = 1e-06
N = 8
F32 = jnp.float32
BF16 = jnp.bfloat16
VMEM_LIMIT = 60 * 1024 * 1024

(
    ROWS_X, COLS_Y, ROWS_Y, COLS_X, D_ROWS_X, D_COLS_Y, D_ROWS_Y, D_COLS_X,
    WEIGHTS, MASKED, CONV, MEANS, DCONV, BRANCH, GAIN, G_X, G_X2, G_Z, G_Y, G_ALL, S_Y, S_X,
) = range(22)


def dot(a, b, dims):
    return lax.dot_general(a, b, (dims, ((), ())), preferred_element_type=F32)


def lanes(t, width=128):
    return pl.ds(pl.multiple_of(t * width, width), width)


def rows16(p):
    return pl.ds(pl.multiple_of(p * 16, 16), 16)


def kernel_body(
    act_h, cot_h, ker_h, gain_h, w_in_h, w_out_h, nbr_h, mask_h,
    out_h, igrad_h, kgrad_h, ggrad_h, w_in_grad_h, w_out_grad_h,
    act, cot, ker, gain, w_in, w_out, nbr, mask,
    out, igrad, kgrad_out, gain_out, w_in_out, w_out_out,
    xpad, dpad, wb, rows, cols, d_rows, d_cols,
    rows_t, cols_t, d_rows_t, d_cols_t, row_masks, col_masks,
    rows_s, cols_s, d_rows_s, d_cols_s, rows_g, cols_g, d_rows_g, d_cols_g,
    outers, sides, fixes, conv_c, back_c, sums,
    weights, masked, conv_r, means, convs, mean_all, dz, normed, feats, act_h2, dpre_h,
    dconv_s, dconv, branch_s, branch, gain_s, gains, g_s, g_x, g_xs, g_z, g_y, g_all, s_y, s_x,
    ssem, rsem, lsem, osem,
):
    tile = lax.axis_index("tile")
    z = lax.axis_index("chan")
    y = tile // N
    q = lax.rem(tile, N)
    mine = {"y": y, "x": q, "z": z}

    def device(group, p):
        if group == "y":
            return (p * N + q, z)
        if group == "x":
            return (y * N + p, z)
        return (tile, p)

    def copy(stage, group, src, dst, to, slot):
        return pltpu.make_async_remote_copy(
            src_ref=src,
            dst_ref=dst,
            send_sem=ssem.at[stage, to],
            recv_sem=rsem.at[stage, slot],
            device_id=device(group, to),
            device_id_type=pl.DeviceIdType.MESH,
        )

    def peers(group, step):
        def one(j, carry):
            step(lax.rem(mine[group] + 4 + (1 - 2 * lax.rem(j, 2)) * ((j + 1) // 2), N))
            return carry

        lax.fori_loop(0, N - 1, one, 0)

    sent = []

    def start(stage, group, src, dst):
        me = mine[group]
        peers(group, lambda p: copy(stage, group, src(p), dst(me), p, me).start())
        sent.append((stage, group, src, dst))

    def arrive(stage, group, src, dst):
        peers(group, lambda p: copy(stage, group, src(p), dst(p), p, p).wait_recv())

    def settle():
        for stage, group, src, dst in sent:
            me = mine[group]
            peers(group, lambda p: copy(stage, group, src(p), dst(me), p, me).wait_send())
        sent.clear()

    lane = lax.broadcasted_iota(jnp.int32, (16, 128), 1)
    lane1 = lax.broadcasted_iota(jnp.int32, (1, 1, 128), 2)
    low = lane < 64
    rest = lane & 63
    edge = (rest < 3) | (rest >= 61)
    beside = ((lane >= 64) & (lane < 67)) | (lane >= 125)

    def window_in(index, members):
        found = index < 0
        for member in members:
            found = found | (index == member)
        return found

    def pair(ref, t):
        return ref[:, lanes(t)].astype(F32)

    def roll(x, shift, axis):
        shift = shift % 128
        return x if shift == 0 else pltpu.roll(x, shift, axis)

    inputs = [
        (act_h, act), (nbr_h, nbr), (cot_h, cot), (mask_h, mask),
        (w_in_h, w_in), (w_out_h, w_out), (ker_h, ker), (gain_h, gain),
    ]
    loads = [pltpu.make_async_copy(src, dst, lsem.at[i]) for i, (src, dst) in enumerate(inputs)]
    results = [
        (out, out_h), (igrad, igrad_h), (kgrad_out, kgrad_h), (gain_out, ggrad_h),
        (w_in_out, w_in_grad_h), (w_out_out, w_out_grad_h),
    ]
    stores = [pltpu.make_async_copy(src, dst, osem.at[i]) for i, (src, dst) in enumerate(results)]

    barrier = pltpu.get_barrier_semaphore()
    for group in ("y", "x", "z"):
        peers(
            group,
            lambda p, group=group: pl.semaphore_signal(
                barrier, inc=1, device_id=device(group, p), device_id_type=pl.DeviceIdType.MESH
            ),
        )
    for load in loads:
        load.start()

    def build_rows(src, dst):
        dst[0:16, :] = src[:, 0:128]
        dst[16:32, :] = jnp.where(low, pair(src, 1), pair(src, 30)).astype(BF16)
        dst[32:48, :] = src[:, 3968:4096]

    def build_cols(src, dst):
        for block in range(4):
            total = jnp.zeros((16, 128), F32)
            for t in range(8):
                total = total + roll(jnp.where(edge, pair(src, block * 8 + t), 0.0), 8 * t, 1)
            dst[16 * block : 16 * block + 16, :] = total.astype(BF16)

    loads[0].wait()
    build_cols(act, cols)
    build_rows(act, rows)
    loads[1].wait()
    eight = lax.broadcasted_iota(jnp.int32, (16, 8), 0) == lax.broadcasted_iota(jnp.int32, (16, 8), 1)
    listed = jnp.sum(
        jnp.where(eight, jnp.broadcast_to(nbr[...].astype(F32), (16, 8)), 0.0), 1, keepdims=True
    )
    listed = jnp.broadcast_to(listed, (16, 128)).astype(BF16)
    rows[48:64, :] = listed
    for k in range(8):
        spare = jnp.broadcast_to(nbr[0:1, k : k + 1].astype(F32), (16, 128)).astype(BF16)
        cols[0:16, :] = jnp.where(lane == 8 * k + 3, spare, cols[0:16, :])

    pl.semaphore_wait(barrier, 3 * (N - 1))
    c1_src, c1_dst = (lambda p: cols), (lambda p: cols_t.at[p])
    start(COLS_Y, "y", c1_src, c1_dst)
    r1_src, r1_dst = (lambda p: rows), (lambda p: rows_t.at[p])
    start(ROWS_X, "x", r1_src, r1_dst)
    cols_t[y] = cols[...]
    rows_t[q] = rows[...]

    for load in loads[2:]:
        load.wait()
    weights[z, 0:64, :] = w_in[...]
    weights[z, 64:128, :] = w_out[...]
    w_src, w_dst = (lambda p: weights.at[z]), (lambda p: weights.at[p])
    start(WEIGHTS, "z", w_src, w_dst)

    def mask_cot(t, carry):
        kept = mask[:, lanes(t, 512)].astype(F32)
        masked[:, lanes(t, 512)] = (cot[:, lanes(t, 512)].astype(F32) * kept).astype(BF16)
        return carry

    lax.fori_loop(0, 8, mask_cot, 0)
    m_src, m_dst = (lambda p: masked.at[:, lanes(p, 512)]), (lambda p: dz.at[rows16(p), :])
    start(MASKED, "z", m_src, m_dst)
    dz[rows16(z), :] = masked[:, lanes(z, 512)]

    for tap in range(49):
        wb[tap] = jnp.broadcast_to(ker[:, tap : tap + 1], (16, 128))

    def spread(src, dst):
        def some(block, carry):
            for u in range(8):
                both = pair(src, 8 * block + u)
                dst[3 + 16 * block + 2 * u] = jnp.where(low, both, 0.0)
                dst[4 + 16 * block + 2 * u] = jnp.where(low, roll(both, 64, 1), 0.0)
            return carry

        for row in (0, 1, 2, 67, 68, 69):
            dst[row] = jnp.zeros((16, 128), F32)
        lax.fori_loop(0, 4, some, 0)

    spread(act, xpad)

    def filtered(src, flip, r):
        total = None
        for b in range(7):
            part = None
            for a in range(7):
                tap = (6 - a) * 7 + 6 - b if flip else a * 7 + b
                term = wb[tap][None] * src[pl.ds(8 * r + a, 8)]
                part = term if part is None else part + term
            part = roll(part, 3 - b, 2)
            total = part if total is None else total + part
        return [jnp.where(low, total[2 * u], roll(total[2 * u + 1], 64, 1)) for u in range(4)]

    def centre(src, flip, dst, first=0, last=N):
        def some(r, carry):
            tiles = filtered(src, flip, r)
            for u in range(4):
                dst[:, lanes(4 * r + u)] = tiles[u]
            return carry

        lax.fori_loop(first, last, some, 0)

    centre(xpad, False, conv_c)

    index4 = lane1 // 4
    odd = (index4 & 1) == 1
    in_top = window_in(index4, (0, 15, 16, 31, 2, 17))
    in_bottom = window_in(index4, (28, 11, 14, 29, 30, 13))

    def make_col_masks(d, carry):
        number = (y * N + d).astype(F32)
        near = (cols_t[:, 0:16, :].astype(F32)[:, 0:1, :] == number).astype(F32)
        m = [jnp.broadcast_to(near[:, :, 8 * k + 3 : 8 * k + 4], (N, 1, 128)) for k in range(8)]
        col_masks[d, :, 0:1, :] = jnp.where(odd, m[4], m[3])
        col_masks[d, :, 1:2, :] = jnp.where(
            in_top, jnp.where(odd, m[2], m[0]), jnp.where(in_bottom, jnp.where(odd, m[7], m[5]), 0.0)
        )
        return carry

    def make_row_masks(d, carry):
        number = (d * N + q).astype(F32)
        near = (rows_t[:, 48:64, :].astype(F32) == number).astype(F32)
        m = [near[:, k : k + 1, :] for k in range(8)]
        row_masks[d, :, 0:1, :] = m[1]
        row_masks[d, :, 1:2, :] = jnp.where(lane1 < 64, m[1], m[6])
        row_masks[d, :, 2:3, :] = m[6]
        return carry

    def choose_rows(src, dst):
        def one(d, carry):
            for part in range(3):
                block = src[:, 16 * part : 16 * part + 16, :].astype(F32)
                total = jnp.sum(row_masks[d, :, part : part + 1, :] * block, 0)
                dst[d, 16 * part : 16 * part + 16, :] = total.astype(BF16)
            return carry

        lax.fori_loop(0, N, one, 0)

    def choose_cols(src, dst):
        def one(d, carry):
            for part in range(4):
                block = src[:, 16 * part : 16 * part + 16, :].astype(F32)
                total = jnp.sum(col_masks[d, :, 0:1, :] * block, 0)
                dst[d, 16 * part : 16 * part + 16, :] = total.astype(BF16)
            block = jnp.where(in_bottom, src[:, 48:64, :].astype(F32), src[:, 0:16, :].astype(F32))
            dst[d, 64:80, :] = jnp.sum(col_masks[d, :, 1:2, :] * block, 0).astype(BF16)
            return carry

        lax.fori_loop(0, N, one, 0)

    def added(me, own, got, i):
        total = own[me, 16 * i : 16 * i + 16, :].astype(F32)
        for j in range(1, N):
            total = total + got[lax.rem(me + j, N), 16 * i : 16 * i + 16, :].astype(F32)
        return total

    block8, in8 = lane1 // 8, lane1 & 7
    place = jnp.where(in8 < 4, (block8 + 8) & 15, (block8 + 1) & 15)
    half, step = jnp.where(place < 8, 1, 0), place & 7

    def gather_halo(own_rows, got_rows, own_cols, got_cols):
        top, mid, end = [added(y, own_rows, got_rows, i) for i in range(3)]
        corner = added(q, own_cols, got_cols, 4)
        centres = (roll(mid, 64, 1), end, roll(end, 64, 1), top, roll(top, 64, 1), mid)
        for i, shift in enumerate((80, 8, 72, 64, 0, 56)):
            outers[i] = jnp.where(low, centres[i], jnp.where(beside, roll(corner, shift, 1), 0.0))
        sides[0] = jnp.zeros((16, 128), F32)
        sides[5] = jnp.zeros((16, 128), F32)
        for block in range(4):
            sides[1 + block] = added(q, own_cols, got_cols, block)

    def fill_pad(dst):
        for i, row in enumerate((0, 1, 2, 67, 68, 69)):
            dst[row] = outers[i]
        for block in range(4):
            side = sides[1 + block]
            for t in range(8):
                for o in range(2):
                    row = 3 + 16 * block + 2 * t + o
                    near = roll(side, 64 * (1 - o) - 8 * t, 1)
                    dst[row] = dst[row] + jnp.where(beside, near, 0.0)

    def fix_rows(flip, dst):
        def fixed(pieces):
            total = None
            for b in range(7):
                part = None
                for a, i in pieces:
                    tap = (6 - a) * 7 + 6 - b if flip else a * 7 + b
                    term = wb[tap] * outers[i]
                    part = term if part is None else part + term
                part = roll(part, 3 - b, 1)
                total = part if total is None else total + part
            return total

        tops = [fixed([(a, i + a) for a in range(3 - i)]) for i in range(3)]
        ends = [fixed([(6 - i + m, 3 + m) for m in range(i + 1)]) for i in range(3)]
        zero = jnp.zeros((16, 128), F32)
        for t, lower, upper in (
            (0, tops[0], tops[1]), (1, tops[2], zero), (30, zero, ends[0]), (31, ends[1], ends[2]),
        ):
            at = slice(128 * t, 128 * t + 128)
            dst[:, at] = dst[:, at] + jnp.where(low, lower, roll(upper, 64, 1))

    def fix_cols(flip):
        for first in (0, 2):
            parts = [None] * 7
            for a in range(7):
                by = a - 3
                moved = sides[first + 1 : first + 3]
                if by:
                    moved = jnp.zeros((2, 16, 128), F32)
                    for o in range(2):
                        up = (o + by) // 2
                        other = (o + by) - 2 * up
                        for over in (-1, 0, 1):
                            if over * up < 0 or (over and not up):
                                continue
                            fits = (half == o) & (step + up >= 8 * over) & (step + up < 8 * over + 8)
                            source = sides[first + 1 + over : first + 3 + over]
                            shift = -8 * (up - 8 * over + 8 * (o - other))
                            moved = jnp.where(fits, roll(source, shift, 2), moved)
                for b in (0, 1, 2, 4, 5, 6):
                    tap = (6 - a) * 7 + 6 - b if flip else a * 7 + b
                    term = wb[tap][None] * moved
                    parts[b] = term if parts[b] is None else parts[b] + term
            total = jnp.zeros((2, 16, 128), F32)
            for b in (0, 1, 2, 4, 5, 6):
                lands = in8 < 3 - b if b < 3 else in8 > 10 - b
                total = total + jnp.where(lands, roll(parts[b], 3 - b, 2), 0.0)
            fixes[first : first + 2] = total

    arrive(ROWS_X, "x", r1_src, r1_dst)
    lax.fori_loop(0, N, make_row_masks, 0)
    choose_rows(rows_t, rows_s)
    r2_src, r2_dst = (lambda p: rows_s.at[p]), (lambda p: rows_g.at[p])
    start(ROWS_Y, "y", r2_src, r2_dst)
    arrive(COLS_Y, "y", c1_src, c1_dst)
    lax.fori_loop(0, N, make_col_masks, 0)
    choose_cols(cols_t, cols_s)
    c2_src, c2_dst = (lambda p: cols_s.at[p]), (lambda p: cols_g.at[p])
    start(COLS_X, "x", c2_src, c2_dst)
    arrive(ROWS_Y, "y", r2_src, r2_dst)
    arrive(COLS_X, "x", c2_src, c2_dst)
    gather_halo(rows_s, rows_g, cols_s, cols_g)
    fix_rows(False, conv_c)
    fix_cols(False)

    c_src, c_dst = (lambda p: conv_r.at[:, lanes(p, 512)]), (lambda p: convs.at[rows16(p), :])
    a_src, a_dst = (lambda p: means.at[:, lanes(p, 512)]), (lambda p: mean_all.at[p])

    def forward(block, carry):
        for t in range(8):
            at = lanes(8 * block + t)
            whole = conv_c[:, at] + jnp.where(edge, roll(fixes[block], 64 - 8 * t, 1), 0.0)
            mean = jnp.sum(whole, 0, keepdims=True) * (1.0 / 16)
            conv_r[:, at] = (whole - mean).astype(BF16)
            means[:, at] = mean
        return carry

    lax.fori_loop(0, 4, forward, 0)
    start(CONV, "z", c_src, c_dst)
    start(MEANS, "z", a_src, a_dst)
    convs[rows16(z), :] = conv_r[:, lanes(z, 512)]
    mean_all[z] = means[:, lanes(z, 512)]
    fill_pad(xpad)
    settle()
    arrive(CONV, "z", c_src, c_dst)
    arrive(MEANS, "z", a_src, a_dst)

    local = mean_all[...]
    mean = jnp.sum(local, 0) * (1.0 / N)
    centred = (convs[...].astype(F32).reshape(N, 16, 512) + (local - mean[None])).reshape(128, 512)
    rstd = lax.rsqrt(jnp.sum(centred * centred, 0, keepdims=True) * (1.0 / 128) + EPS)
    normed[...] = centred * rstd
    diagonal = lax.broadcasted_iota(jnp.int32, (128, 128), 0) == lax.broadcasted_iota(
        jnp.int32, (128, 128), 1
    )
    gain_col = jnp.sum(jnp.where(diagonal, jnp.broadcast_to(gain[...], (128, 128)), 0.0), 1, keepdims=True)
    feats[...] = (normed[...] * gain_col).astype(BF16)
    arrive(WEIGHTS, "z", w_src, w_dst)
    arrive(MASKED, "z", m_src, m_dst)

    def hidden(g, carry):
        wi = weights[pl.ds(2 * g, 2), 0:64, :].reshape(128, 128)
        wo = weights[pl.ds(2 * g, 2), 64:128, :].reshape(128, 128)
        pre = dot(wi, feats[...], ((1,), (0,)))
        square = pre * pre
        bend = jnp.tanh(0.7978845608 * pre * (1.0 + 0.044715 * square))
        half = 0.5 + 0.5 * bend
        act_h2[lanes(g), :] = (pre * half).astype(BF16)
        slope = half + (0.5 * 0.7978845608) * pre * (1.0 - bend * bend) * (
            1.0 + (3.0 * 0.044715) * square
        )
        d_act = dot(wo, dz[...], ((1,), (0,)))
        dpre_h[lanes(g), :] = (d_act * slope).astype(BF16)
        return carry

    def weight_grads(part, stage):
        units, groups = slice(256 * part, 256 * part + 256), pl.ds(4 * part, 4)
        g_s[groups, 0:64, :] = dot(dpre_h[units, :], feats[...], ((1,), (1,))).astype(BF16).reshape(4, 64, 128)
        g_s[groups, 64:128, :] = dot(act_h2[units, :], dz[...], ((1,), (1,))).astype(BF16).reshape(4, 64, 128)
        src, dst = (lambda p: g_s.at[groups, rows16(p), :]), (lambda p: g_x.at[p, groups])
        start(stage, "x", src, dst)
        return src, dst

    lax.fori_loop(0, 2, hidden, 0)
    gx_src, gx_dst = weight_grads(0, G_X)
    lax.fori_loop(2, 4, hidden, 0)
    wi_all = weights[:, 0:64, :].reshape(512, 128)
    wo_all = weights[:, 64:128, :].reshape(512, 128)
    d_feat = dot(wi_all, dpre_h[...], ((0,), (0,)))
    per_gain = d_feat * normed[...]
    d_norm = d_feat * gain_col
    first = jnp.sum(d_norm, 0, keepdims=True) * (1.0 / 128)
    second = jnp.sum(per_gain * gain_col, 0, keepdims=True) * (1.0 / 128)
    dconv_s[...] = (rstd * (d_norm - first - normed[...] * second)).astype(BF16)
    d_src, d_dst = (lambda p: dconv_s.at[rows16(p), :]), (lambda p: dconv.at[:, lanes(p, 512)])
    start(DCONV, "z", d_src, d_dst)
    dconv[:, lanes(z, 512)] = dconv_s[rows16(z), :]
    gx2_src, gx2_dst = weight_grads(1, G_X2)
    g_x[q] = g_s[:, rows16(q), :]
    gain_sum = jnp.sum(per_gain, 1, keepdims=True)
    gain_s[...] = jnp.sum(jnp.where(diagonal, gain_sum, 0.0), 0, keepdims=True)
    n_src, n_dst = (lambda p: gain_s), (lambda p: gains.at[p])
    start(GAIN, "z", n_src, n_dst)
    gains[z] = gain_s[...]

    branch_s[...] = dot(wo_all, act_h2[...], ((0,), (0,))).astype(BF16)
    branch[:, lanes(z, 512)] = branch_s[rows16(z), :]
    arrive(G_X, "x", gx_src, gx_dst)
    arrive(G_X2, "x", gx2_src, gx2_dst)
    g_xs[...] = jnp.sum(g_x[...].astype(F32), 0).astype(BF16)
    gz_src, gz_dst = (lambda p: g_xs.at[p]), (lambda p: g_z.at[p])
    start(G_Z, "z", gz_src, gz_dst)
    g_z[z] = g_xs[z]
    arrive(DCONV, "z", d_src, d_dst)
    build_cols(dconv, d_cols)
    e1_src, e1_dst = (lambda p: d_cols), (lambda p: d_cols_t.at[p])
    start(D_COLS_Y, "y", e1_src, e1_dst)
    build_rows(dconv, d_rows)
    f1_src, f1_dst = (lambda p: d_rows), (lambda p: d_rows_t.at[p])
    start(D_ROWS_X, "x", f1_src, f1_dst)
    d_cols_t[y] = d_cols[...]
    d_rows_t[q] = d_rows[...]

    spread(dconv, dpad)

    def taps(r, carry):
        for b in range(7):
            moved = roll(dpad[pl.ds(3 + 8 * r, 8)], b - 3, 2)
            for a in range(7):
                sums[a * 7 + b] += jnp.sum(moved * xpad[pl.ds(8 * r + a, 8)], 0)
        return carry

    sums[...] = jnp.zeros((49, 16, 128), F32)
    lax.fori_loop(0, 8, taps, 0)
    small = jnp.zeros((16, 128), F32)
    for tap in range(49):
        small = jnp.where(lane == tap, jnp.sum(sums[tap], 1, keepdims=True), small)
    arrive(GAIN, "z", n_src, n_dst)
    sub = lax.broadcasted_iota(jnp.int32, (16, 128), 0)
    gain_mine = jnp.where(lane == sub + 16 * z, jnp.broadcast_to(jnp.sum(gains[...], 0), (16, 128)), 0.0)
    small = jnp.where(lane == 49, jnp.sum(gain_mine, 1, keepdims=True), small)
    s_y[y] = small
    sy_src, sy_dst = (lambda p: s_y.at[y]), (lambda p: s_y.at[p])
    start(S_Y, "y", sy_src, sy_dst)

    arrive(G_Z, "z", gz_src, gz_dst)
    g_y[y] = jnp.sum(g_z[...].astype(F32), 0)
    gy_src, gy_dst = (lambda p: g_y.at[y]), (lambda p: g_y.at[p])
    start(G_Y, "y", gy_src, gy_dst)
    arrive(D_ROWS_X, "x", f1_src, f1_dst)
    choose_rows(d_rows_t, d_rows_s)
    f2_src, f2_dst = (lambda p: d_rows_s.at[p]), (lambda p: d_rows_g.at[p])
    start(D_ROWS_Y, "y", f2_src, f2_dst)
    arrive(D_COLS_Y, "y", e1_src, e1_dst)
    choose_cols(d_cols_t, d_cols_s)
    e2_src, e2_dst = (lambda p: d_cols_s.at[p]), (lambda p: d_cols_g.at[p])
    start(D_COLS_X, "x", e2_src, e2_dst)
    b_src, b_dst = (lambda p: branch_s.at[rows16(p), :]), (lambda p: branch.at[:, lanes(p, 512)])
    start(BRANCH, "z", b_src, b_dst)
    centre(dpad, True, back_c, 0, 4)
    arrive(S_Y, "y", sy_src, sy_dst)
    s_x[q] = jnp.sum(s_y[...], 0)
    sx_src, sx_dst = (lambda p: s_x.at[q]), (lambda p: s_x.at[p])
    start(S_X, "x", sx_src, sx_dst)
    centre(dpad, True, back_c, 4, N)
    arrive(G_Y, "y", gy_src, gy_dst)
    g_all[q] = jnp.sum(g_y[...], 0)
    ga_src, ga_dst = (lambda p: g_all.at[q]), (lambda p: g_all.at[p])
    start(G_ALL, "x", ga_src, ga_dst)

    arrive(D_ROWS_Y, "y", f2_src, f2_dst)
    arrive(D_COLS_X, "x", e2_src, e2_dst)
    gather_halo(d_rows_s, d_rows_g, d_cols_s, d_cols_g)
    fix_rows(True, back_c)
    fix_cols(True)

    def backward(block, carry):
        for t in range(8):
            at = lanes(8 * block + t)
            whole = back_c[:, at] + jnp.where(edge, roll(fixes[block], 64 - 8 * t, 1), 0.0)
            igrad[:, at] = (cot[:, at].astype(F32) + whole).astype(BF16)
        return carry

    lax.fori_loop(0, 4, backward, 0)
    stores[1].start()

    arrive(BRANCH, "z", b_src, b_dst)

    def write_out(t, carry):
        at = lanes(t, 512)
        kept = mask[:, at].astype(F32)
        out[:, at] = (act[:, at].astype(F32) + kept * branch[:, at].astype(F32)).astype(BF16)
        return carry

    lax.fori_loop(0, 8, write_out, 0)
    stores[0].start()

    settle()
    arrive(S_X, "x", sx_src, sx_dst)
    small = jnp.sum(s_x[...], 0)
    kgrad_out[...] = small[:, 0:49]
    square16 = lax.broadcasted_iota(jnp.int32, (16, 16), 0) == lax.broadcasted_iota(
        jnp.int32, (16, 16), 1
    )
    gain_out[...] = jnp.sum(
        jnp.where(square16, jnp.broadcast_to(small[:, 49:50], (16, 16)), 0.0), 0, keepdims=True
    )
    stores[2].start()
    stores[3].start()
    arrive(G_ALL, "x", ga_src, ga_dst)
    both = g_all[...].reshape(128, 128)
    w_in_out[...] = both[0:64]
    w_out_out[...] = both[64:128]
    stores[4].start()
    stores[5].start()
    settle()
    for store in stores:
        store.wait()


def finish_body(*refs):
    count = (len(refs) - 2) // 3
    arrays, results, held = refs[:count], refs[count : 2 * count], refs[2 * count : 3 * count]
    came, went = refs[-2:]
    loads = [pltpu.make_async_copy(arrays[i], held[i], came.at[i]) for i in range(count)]
    stores = [pltpu.make_async_copy(held[i], results[i], went.at[i]) for i in range(count)]
    for load in loads:
        load.start()
    for load, store in zip(loads, stores):
        load.wait()
        store.start()
    for store in stores:
        store.wait()


def body(activations, cotangent, kernel, gain, w_in, w_out, neighbours, land_mask):
    anywhere = pl.BlockSpec(memory_space=pl.ANY)
    scratch = [
        ((16, 4096), BF16),
        ((16, 4096), BF16),
        ((16, 49), F32),
        ((1, 128), F32),
        ((64, 128), BF16),
        ((64, 128), BF16),
        ((1, 8), jnp.int32),
        ((1, 4096), jnp.int32),
        ((16, 4096), BF16),
        ((16, 4096), BF16),
        ((16, 49), F32),
        ((1, 16), F32),
        ((64, 128), F32),
        ((64, 128), F32),
        ((70, 16, 128), F32),
        ((70, 16, 128), F32),
        ((49, 16, 128), F32),
        ((64, 128), BF16),
        ((64, 128), BF16),
        ((48, 128), BF16),
        ((64, 128), BF16),
        ((N, 64, 128), BF16),
        ((N, 64, 128), BF16),
        ((N, 48, 128), BF16),
        ((N, 64, 128), BF16),
        ((N, N, 8, 128), F32),
        ((N, N, 8, 128), F32),
        ((N, 48, 128), BF16),
        ((N, 80, 128), BF16),
        ((N, 48, 128), BF16),
        ((N, 80, 128), BF16),
        ((N, 48, 128), BF16),
        ((N, 80, 128), BF16),
        ((N, 48, 128), BF16),
        ((N, 80, 128), BF16),
        ((6, 16, 128), F32),
        ((6, 16, 128), F32),
        ((4, 16, 128), F32),
        ((16, 4096), F32),
        ((16, 4096), F32),
        ((49, 16, 128), F32),
        ((N, 128, 128), BF16),
        ((16, 4096), BF16),
        ((16, 4096), BF16),
        ((1, 4096), F32),
        ((128, 512), BF16),
        ((N, 1, 512), F32),
        ((128, 512), BF16),
        ((128, 512), F32),
        ((128, 512), BF16),
        ((512, 512), BF16),
        ((512, 512), BF16),
        ((128, 512), BF16),
        ((16, 4096), BF16),
        ((128, 512), BF16),
        ((16, 4096), BF16),
        ((1, 128), F32),
        ((N, 1, 128), F32),
        ((N, 128, 128), BF16),
        ((N, N, 16, 128), BF16),
        ((N, 16, 128), BF16),
        ((N, 16, 128), BF16),
        ((N, 16, 128), F32),
        ((N, 16, 128), F32),
        ((N, 16, 128), F32),
        ((N, 16, 128), F32),
    ]
    shapes = [
        jax.ShapeDtypeStruct((16, 4096), BF16),
        jax.ShapeDtypeStruct((16, 4096), BF16),
        jax.ShapeDtypeStruct((16, 49), F32),
        jax.ShapeDtypeStruct((1, 16), F32),
        jax.ShapeDtypeStruct((64, 128), F32),
        jax.ShapeDtypeStruct((64, 128), F32),
    ]
    results = pl.pallas_call(
        kernel_body,
        out_shape=shapes,
        in_specs=[anywhere] * 8,
        out_specs=[anywhere] * 6,
        scratch_shapes=[pltpu.VMEM(shape, kind) for shape, kind in scratch]
        + [
            pltpu.SemaphoreType.DMA((22, N)),
            pltpu.SemaphoreType.DMA((22, N)),
            pltpu.SemaphoreType.DMA((8,)),
            pltpu.SemaphoreType.DMA((6,)),
        ],
        compiler_params=pltpu.CompilerParams(
            collective_id=0, has_side_effects=True, vmem_limit_bytes=VMEM_LIMIT
        ),
        cost_estimate=pl.CostEstimate(flops=360000000, bytes_accessed=1000000, transcendentals=262144),
        name="block",
    )(
        activations[0], cotangent[0], kernel, gain.reshape(1, 128), w_in.T, w_out, neighbours, land_mask,
    )
    out, igrad, kgrad, ggrad, wigrad, wograd = pl.pallas_call(
        finish_body,
        out_shape=shapes,
        in_specs=[anywhere] * 6,
        out_specs=[anywhere] * 6,
        scratch_shapes=[pltpu.VMEM(result.shape, result.dtype) for result in shapes]
        + [pltpu.SemaphoreType.DMA((6,)), pltpu.SemaphoreType.DMA((6,))],
        compiler_params=pltpu.CompilerParams(vmem_limit_bytes=VMEM_LIMIT),
        name="results",
    )(*results)
    return (out[None], igrad[None], kgrad, ggrad.reshape(16), wigrad.T, wograd)


def solution(mesh):
    placed = (
        P("tile", "chan", None),
        P("tile", "chan", None),
        P("chan", None),
        P(),
        P(None, "chan"),
        P("chan", None),
        P("tile", None),
        P("tile", None),
    )
    return jax.shard_map(
        body,
        mesh=mesh,
        in_specs=placed,
        out_specs=(
            P("tile", "chan", None),
            P("tile", "chan", None),
            P("chan", None),
            P("chan"),
            P(None, "chan"),
            P("chan", None),
        ),
        check_vma=False,
    )
```

```python
import jax
import jax.numpy as jnp
from jax import lax
from jax.experimental import pallas as pl
from jax.experimental.pallas import tpu as pltpu
from jax.sharding import PartitionSpec as P

EPS = 1e-06
N = 8
F32 = jnp.float32
BF16 = jnp.bfloat16
VMEM_LIMIT = 60 * 1024 * 1024

(
    ROWS_X, COLS_Y, ROWS_Y, COLS_X, D_ROWS_X, D_COLS_Y, D_ROWS_Y, D_COLS_X,
    WEIGHTS, MASKED, CONV, MEANS, DCONV, BRANCH, GAIN, G_X, G_X2, G_Z, G_Y, G_ALL, S_Y, S_X,
    FIX_COLS, FIX_ROWS, SIBLING,
) = range(25)


def dot(a, b, dims):
    return lax.dot_general(a, b, (dims, ((), ())), preferred_element_type=F32)


def lanes(t, width=128):
    return pl.ds(pl.multiple_of(t * width, width), width)


def rows16(p):
    return pl.ds(pl.multiple_of(p * 16, 16), 16)


def kernel_body(
    act_h, cot_h, ker_h, gain_h, w_in_h, w_out_h, nbr_h, mask_h,
    out_h, igrad_h, kgrad_h, ggrad_h, w_in_grad_h, w_out_grad_h,
    act, cot, ker, gain, w_in, w_out, nbr, mask,
    out, igrad, kgrad_out, gain_out, w_in_out, w_out_out,
    xpad, dpad, wb, rows, cols, d_rows, d_cols,
    rows_t, cols_t, d_rows_t, d_cols_t, row_masks, col_masks,
    rows_s, cols_s, d_rows_s, d_cols_s, rows_g, cols_g, d_rows_g, d_cols_g,
    outers, sides, fixes, row_fix, fix_g, row_fix_g, added_in, back_c, sums,
    weights, masked, conv_r, means, convs, mean_all, dz, normed, feats, act_h2, dpre_h,
    dconv_s, dconv, branch_s, branch, gain_s, gains, g_s, g_x, g_xs, g_z, g_y, g_all, s_y, s_x,
    ssem, rsem, lsem, osem,
):
    tile = lax.axis_index("tile")
    z = lax.axis_index("chan")
    y = tile // N
    q = lax.rem(tile, N)
    mine = {"y": y, "x": q, "z": z}

    def device(group, p):
        if group == "y":
            return (p * N + q, z)
        if group == "x":
            return (y * N + p, z)
        return (tile, p)

    def copy(stage, group, src, dst, to, slot):
        return pltpu.make_async_remote_copy(
            src_ref=src,
            dst_ref=dst,
            send_sem=ssem.at[stage, to],
            recv_sem=rsem.at[stage, slot],
            device_id=device(group, to),
            device_id_type=pl.DeviceIdType.MESH,
        )

    def peers(group, step):
        for offset in (4, 3, 5, 2, 6, 1, 7):
            step((mine[group] + offset) & (N - 1))

    sent = []

    def start(stage, group, src, dst):
        me = mine[group]
        peers(group, lambda p: copy(stage, group, src(p), dst(me), p, me).start())
        sent.append((stage, group, src, dst))

    def arrive(stage, group, src, dst):
        peers(group, lambda p: copy(stage, group, src(p), dst(p), p, p).wait_recv())

    def settle():
        for stage, group, src, dst in sent:
            me = mine[group]
            peers(group, lambda p: copy(stage, group, src(p), dst(me), p, me).wait_send())
        sent.clear()

    lane = lax.broadcasted_iota(jnp.int32, (16, 128), 1)
    lane1 = lax.broadcasted_iota(jnp.int32, (1, 1, 128), 2)
    low = lane < 64
    rest = lane & 63
    edge = (rest < 3) | (rest >= 61)
    beside = ((lane >= 64) & (lane < 67)) | (lane >= 125)

    def window_in(index, members):
        found = index < 0
        for member in members:
            found = found | (index == member)
        return found

    def pair(ref, t):
        return ref[:, lanes(t)].astype(F32)

    def roll(x, shift, axis):
        shift = shift % 128
        return x if shift == 0 else pltpu.roll(x, shift, axis)

    inputs = [
        (act_h, act), (nbr_h, nbr), (cot_h, cot), (mask_h, mask),
        (w_in_h, w_in), (w_out_h, w_out), (ker_h, ker), (gain_h, gain),
    ]
    loads = [pltpu.make_async_copy(src, dst, lsem.at[i]) for i, (src, dst) in enumerate(inputs)]
    results = [
        (out, out_h), (igrad, igrad_h), (kgrad_out, kgrad_h), (gain_out, ggrad_h),
        (w_in_out, w_in_grad_h), (w_out_out, w_out_grad_h),
    ]
    stores = [pltpu.make_async_copy(src, dst, osem.at[i]) for i, (src, dst) in enumerate(results)]

    barrier = pltpu.get_barrier_semaphore()
    for group in ("y", "x", "z"):
        peers(
            group,
            lambda p, group=group: pl.semaphore_signal(
                barrier, inc=1, device_id=device(group, p), device_id_type=pl.DeviceIdType.MESH
            ),
        )
    for load in loads:
        load.start()

    def build_rows(src, dst):
        dst[0:16, :] = src[:, 0:128]
        dst[16:32, :] = jnp.where(low, pair(src, 1), pair(src, 30)).astype(BF16)
        dst[32:48, :] = src[:, 3968:4096]

    def build_cols(src, dst):
        for block in range(4):
            total = jnp.zeros((16, 128), F32)
            for t in range(8):
                total = total + roll(jnp.where(edge, pair(src, block * 8 + t), 0.0), 8 * t, 1)
            dst[16 * block : 16 * block + 16, :] = total.astype(BF16)

    loads[0].wait()
    build_cols(act, cols)
    build_rows(act, rows)
    loads[1].wait()
    eight = lax.broadcasted_iota(jnp.int32, (16, 8), 0) == lax.broadcasted_iota(jnp.int32, (16, 8), 1)
    listed = jnp.sum(
        jnp.where(eight, jnp.broadcast_to(nbr[...].astype(F32), (16, 8)), 0.0), 1, keepdims=True
    )
    listed = jnp.broadcast_to(listed, (16, 128)).astype(BF16)
    rows[48:64, :] = listed
    for k in range(8):
        spare = jnp.broadcast_to(nbr[0:1, k : k + 1].astype(F32), (16, 128)).astype(BF16)
        cols[0:16, :] = jnp.where(lane == 8 * k + 3, spare, cols[0:16, :])

    pl.semaphore_wait(barrier, 3 * (N - 1))
    c1_src, c1_dst = (lambda p: cols), (lambda p: cols_t.at[p])
    start(COLS_Y, "y", c1_src, c1_dst)
    r1_src, r1_dst = (lambda p: rows), (lambda p: rows_t.at[p])
    start(ROWS_X, "x", r1_src, r1_dst)
    cols_t[y] = cols[...]
    rows_t[q] = rows[...]

    for load in loads[2:]:
        load.wait()
    core = q & 1
    mine_half = pl.ds(pl.multiple_of(64 * core, 64), 64)
    weights[z, mine_half, :] = jnp.where(core == 0, w_in[...], w_out[...])
    w_src, w_dst = (lambda p: weights.at[z, mine_half]), (lambda p: weights.at[p, mine_half])
    start(WEIGHTS, "z", w_src, w_dst)

    def sibling(half, slot):
        part = weights.at[:, half]
        return copy(SIBLING, "x", part, part, q ^ 1, slot)

    def mask_cot(t, carry):
        kept = mask[:, lanes(t, 512)].astype(F32)
        masked[:, lanes(t, 512)] = (cot[:, lanes(t, 512)].astype(F32) * kept).astype(BF16)
        return carry

    lax.fori_loop(0, 8, mask_cot, 0)
    m_src, m_dst = (lambda p: masked.at[:, lanes(p, 512)]), (lambda p: dz.at[rows16(p), :])
    start(MASKED, "z", m_src, m_dst)
    dz[rows16(z), :] = masked[:, lanes(z, 512)]

    for tap in range(49):
        wb[tap] = jnp.broadcast_to(ker[:, tap : tap + 1], (16, 128))

    def spread(src, dst):
        def some(block, carry):
            for u in range(8):
                both = pair(src, 8 * block + u)
                dst[3 + 16 * block + 2 * u] = jnp.where(low, both, 0.0)
                dst[4 + 16 * block + 2 * u] = jnp.where(low, roll(both, 64, 1), 0.0)
            return carry

        for row in (0, 1, 2, 67, 68, 69):
            dst[row] = jnp.zeros((16, 128), F32)
        lax.fori_loop(0, 4, some, 0)

    spread(act, xpad)

    def filtered(src, flip, r):
        total = None
        for b in range(7):
            part = None
            for a in range(7):
                tap = (6 - a) * 7 + 6 - b if flip else a * 7 + b
                term = wb[tap][None] * src[pl.ds(8 * r + a, 8)]
                part = term if part is None else part + term
            part = roll(part, 3 - b, 2)
            total = part if total is None else total + part
        return [jnp.where(low, total[2 * u], roll(total[2 * u + 1], 64, 1)) for u in range(4)]

    def centre(src, flip, dst, first=0, last=N):
        def some(r, carry):
            tiles = filtered(src, flip, r)
            for u in range(4):
                dst[:, lanes(4 * r + u)] = tiles[u]
            return carry

        lax.fori_loop(first, last, some, 0)

    def forward(r, carry):
        tiles = filtered(xpad, False, r)
        for u in range(4):
            mean = jnp.sum(tiles[u], 0, keepdims=True) * (1.0 / 16)
            conv_r[:, lanes(4 * r + u)] = (tiles[u] - mean).astype(BF16)
            means[:, lanes(4 * r + u)] = mean
        return carry

    lax.fori_loop(0, N, forward, 0)
    c_src, c_dst = (lambda p: conv_r.at[:, lanes(p, 512)]), (lambda p: convs.at[rows16(p), :])
    a_src, a_dst = (lambda p: means.at[:, lanes(p, 512)]), (lambda p: mean_all.at[p])
    start(CONV, "z", c_src, c_dst)
    start(MEANS, "z", a_src, a_dst)
    convs[rows16(z), :] = conv_r[:, lanes(z, 512)]
    mean_all[z] = means[:, lanes(z, 512)]

    index4 = lane1 // 4
    odd = (index4 & 1) == 1
    in_top = window_in(index4, (0, 15, 16, 31, 2, 17))
    in_bottom = window_in(index4, (28, 11, 14, 29, 30, 13))

    def make_col_masks(d, carry):
        number = (y * N + d).astype(F32)
        near = (cols_t[:, 0:16, :].astype(F32)[:, 0:1, :] == number).astype(F32)
        m = [jnp.broadcast_to(near[:, :, 8 * k + 3 : 8 * k + 4], (N, 1, 128)) for k in range(8)]
        col_masks[d, :, 0:1, :] = jnp.where(odd, m[4], m[3])
        col_masks[d, :, 1:2, :] = jnp.where(
            in_top, jnp.where(odd, m[2], m[0]), jnp.where(in_bottom, jnp.where(odd, m[7], m[5]), 0.0)
        )
        return carry

    def make_row_masks(d, carry):
        number = (d * N + q).astype(F32)
        near = (rows_t[:, 48:64, :].astype(F32) == number).astype(F32)
        m = [near[:, k : k + 1, :] for k in range(8)]
        row_masks[d, :, 0:1, :] = m[1]
        row_masks[d, :, 1:2, :] = jnp.where(lane1 < 64, m[1], m[6])
        row_masks[d, :, 2:3, :] = m[6]
        return carry

    def choose_rows(src, dst):
        def one(d, carry):
            for part in range(3):
                block = src[:, 16 * part : 16 * part + 16, :].astype(F32)
                total = jnp.sum(row_masks[d, :, part : part + 1, :] * block, 0)
                dst[d, 16 * part : 16 * part + 16, :] = total.astype(BF16)
            return carry

        lax.fori_loop(0, N, one, 0)

    def choose_cols(src, dst):
        def one(d, carry):
            for part in range(4):
                block = src[:, 16 * part : 16 * part + 16, :].astype(F32)
                total = jnp.sum(col_masks[d, :, 0:1, :] * block, 0)
                dst[d, 16 * part : 16 * part + 16, :] = total.astype(BF16)
            block = jnp.where(in_bottom, src[:, 48:64, :].astype(F32), src[:, 0:16, :].astype(F32))
            dst[d, 64:80, :] = jnp.sum(col_masks[d, :, 1:2, :] * block, 0).astype(BF16)
            return carry

        lax.fori_loop(0, N, one, 0)

    def added(me, own, got, i):
        total = own[me, 16 * i : 16 * i + 16, :].astype(F32)
        for j in range(1, N):
            total = total + got[lax.rem(me + j, N), 16 * i : 16 * i + 16, :].astype(F32)
        return total

    block8, in8 = lane1 // 8, lane1 & 7
    place = jnp.where(in8 < 4, (block8 + 8) & 15, (block8 + 1) & 15)
    half, step = jnp.where(place < 8, 1, 0), place & 7

    def gather_halo(own_rows, got_rows, own_cols, got_cols):
        top, mid, end = [added(y, own_rows, got_rows, i) for i in range(3)]
        corner = added(q, own_cols, got_cols, 4)
        centres = (roll(mid, 64, 1), end, roll(end, 64, 1), top, roll(top, 64, 1), mid)
        for i, shift in enumerate((80, 8, 72, 64, 0, 56)):
            outers[i] = jnp.where(low, centres[i], jnp.where(beside, roll(corner, shift, 1), 0.0))
        sides[0] = jnp.zeros((16, 128), F32)
        sides[5] = jnp.zeros((16, 128), F32)
        for block in range(4):
            sides[1 + block] = added(q, own_cols, got_cols, block)

    def fill_pad(dst):
        for i, row in enumerate((0, 1, 2, 67, 68, 69)):
            dst[row] = outers[i]
        for block in range(4):
            side = sides[1 + block]
            for t in range(8):
                for o in range(2):
                    row = 3 + 16 * block + 2 * t + o
                    near = roll(side, 64 * (1 - o) - 8 * t, 1)
                    dst[row] = dst[row] + jnp.where(beside, near, 0.0)

    def fix_rows(flip):
        def fixed(pieces):
            total = None
            for b in range(7):
                part = None
                for a, i in pieces:
                    tap = (6 - a) * 7 + 6 - b if flip else a * 7 + b
                    term = wb[tap] * outers[i]
                    part = term if part is None else part + term
                part = roll(part, 3 - b, 1)
                total = part if total is None else total + part
            return total

        tops = [fixed([(a, i + a) for a in range(3 - i)]) for i in range(3)]
        ends = [fixed([(6 - i + m, 3 + m) for m in range(i + 1)]) for i in range(3)]
        zero = jnp.zeros((16, 128), F32)
        return [
            jnp.where(low, lower, roll(upper, 64, 1))
            for lower, upper in ((tops[0], tops[1]), (tops[2], zero), (zero, ends[0]), (ends[1], ends[2]))
        ]

    def fix_cols(flip):
        for first in (0, 2):
            parts = [None] * 7
            for a in range(7):
                by = a - 3
                moved = sides[first + 1 : first + 3]
                if by:
                    moved = jnp.zeros((2, 16, 128), F32)
                    for o in range(2):
                        up = (o + by) // 2
                        other = (o + by) - 2 * up
                        for over in (-1, 0, 1):
                            if over * up < 0 or (over and not up):
                                continue
                            fits = (half == o) & (step + up >= 8 * over) & (step + up < 8 * over + 8)
                            source = sides[first + 1 + over : first + 3 + over]
                            shift = -8 * (up - 8 * over + 8 * (o - other))
                            moved = jnp.where(fits, roll(source, shift, 2), moved)
                for b in (0, 1, 2, 4, 5, 6):
                    tap = (6 - a) * 7 + 6 - b if flip else a * 7 + b
                    term = wb[tap][None] * moved
                    parts[b] = term if parts[b] is None else parts[b] + term
            total = jnp.zeros((2, 16, 128), F32)
            for b in (0, 1, 2, 4, 5, 6):
                lands = in8 < 3 - b if b < 3 else in8 > 10 - b
                total = total + jnp.where(lands, roll(parts[b], 3 - b, 2), 0.0)
            fixes[first : first + 2] = total

    arrive(ROWS_X, "x", r1_src, r1_dst)
    lax.fori_loop(0, N, make_row_masks, 0)
    choose_rows(rows_t, rows_s)
    r2_src, r2_dst = (lambda p: rows_s.at[p]), (lambda p: rows_g.at[p])
    start(ROWS_Y, "y", r2_src, r2_dst)
    arrive(COLS_Y, "y", c1_src, c1_dst)
    lax.fori_loop(0, N, make_col_masks, 0)
    choose_cols(cols_t, cols_s)
    c2_src, c2_dst = (lambda p: cols_s.at[p]), (lambda p: cols_g.at[p])
    start(COLS_X, "x", c2_src, c2_dst)
    arrive(WEIGHTS, "z", w_src, w_dst)
    sibling(mine_half, q).start()
    arrive(ROWS_Y, "y", r2_src, r2_dst)
    arrive(COLS_X, "x", c2_src, c2_dst)
    gather_halo(rows_s, rows_g, cols_s, cols_g)
    fix_cols(False)
    k_src, k_dst = (lambda p: fixes.at[p // 2]), (lambda p: fix_g.at[rows16(p), :])
    start(FIX_COLS, "z", k_src, k_dst)
    for i, tile_fix in enumerate(fix_rows(False)):
        row_fix[i // 2, :, 128 * (i % 2) : 128 * (i % 2) + 128] = tile_fix

    def row_copy(end, slot):
        return copy(FIX_ROWS, "z", row_fix.at[end], row_fix_g.at[slot], (N - 1) * end, slot)

    for end in range(2):

        @pl.when(z != (N - 1) * end)
        def _():
            row_copy(end, z).start()

    fill_pad(xpad)
    settle()
    for end in range(2):

        @pl.when(z != (N - 1) * end)
        def _():
            row_copy(end, z).wait_send()

    sibling(mine_half, q).wait_send()
    sibling(pl.ds(pl.multiple_of(64 - 64 * core, 64), 64), q ^ 1).wait_recv()
    fix_g[rows16(z), :] = fixes[z // 2]
    arrive(CONV, "z", c_src, c_dst)
    arrive(MEANS, "z", a_src, a_dst)
    arrive(FIX_COLS, "z", k_src, k_dst)
    turned = pltpu.roll(fix_g[...], lax.rem(128 - 32 * (z & 1), 128), 1)
    border = edge[0:1, :]
    for u in range(4):
        added_in[:, 128 * u : 128 * u + 128] = jnp.where(border, roll(turned, 64 - 8 * u, 1), 0.0)
    for end in range(2):

        @pl.when(z == (N - 1) * end)
        def _():
            row_fix_g[z] = row_fix[end]
            peers("z", lambda p: row_copy(end, p).wait_recv())
            at = slice(256 * end, 256 * end + 256)
            added_in[:, at] = added_in[:, at] + row_fix_g[...].reshape(128, 256)

    local = mean_all[...]
    extra = added_in[...]
    mean = jnp.sum(local, 0) * (1.0 / N) + jnp.sum(extra, 0, keepdims=True) * (1.0 / 128)
    centred = (convs[...].astype(F32) + extra).reshape(N, 16, 512) + (local - mean[None])
    centred = centred.reshape(128, 512)
    rstd = lax.rsqrt(jnp.sum(centred * centred, 0, keepdims=True) * (1.0 / 128) + EPS)
    normed[...] = centred * rstd
    diagonal = lax.broadcasted_iota(jnp.int32, (128, 128), 0) == lax.broadcasted_iota(
        jnp.int32, (128, 128), 1
    )
    gain_col = jnp.sum(jnp.where(diagonal, jnp.broadcast_to(gain[...], (128, 128)), 0.0), 1, keepdims=True)
    feats[...] = (normed[...] * gain_col).astype(BF16)
    arrive(MASKED, "z", m_src, m_dst)

    def hidden(g, carry):
        wi = weights[pl.ds(2 * g, 2), 0:64, :].reshape(128, 128)
        wo = weights[pl.ds(2 * g, 2), 64:128, :].reshape(128, 128)
        pre = dot(wi, feats[...], ((1,), (0,)))
        square = pre * pre
        bend = jnp.tanh(0.7978845608 * pre * (1.0 + 0.044715 * square))
        half = 0.5 + 0.5 * bend
        act_h2[lanes(g), :] = (pre * half).astype(BF16)
        slope = half + (0.5 * 0.7978845608) * pre * (1.0 - bend * bend) * (
            1.0 + (3.0 * 0.044715) * square
        )
        d_act = dot(wo, dz[...], ((1,), (0,)))
        dpre_h[lanes(g), :] = (d_act * slope).astype(BF16)
        return carry

    def weight_grads(part, stage):
        units, groups = slice(256 * part, 256 * part + 256), pl.ds(4 * part, 4)
        g_s[groups, 0:64, :] = dot(dpre_h[units, :], feats[...], ((1,), (1,))).astype(BF16).reshape(4, 64, 128)
        g_s[groups, 64:128, :] = dot(act_h2[units, :], dz[...], ((1,), (1,))).astype(BF16).reshape(4, 64, 128)
        src, dst = (lambda p: g_s.at[groups, rows16(p), :]), (lambda p: g_x.at[p, groups])
        start(stage, "x", src, dst)
        return src, dst

    lax.fori_loop(0, 2, hidden, 0)
    gx_src, gx_dst = weight_grads(0, G_X)
    lax.fori_loop(2, 4, hidden, 0)
    wi_all = weights[:, 0:64, :].reshape(512, 128)
    wo_all = weights[:, 64:128, :].reshape(512, 128)
    d_feat = dot(wi_all, dpre_h[...], ((0,), (0,)))
    per_gain = d_feat * normed[...]
    d_norm = d_feat * gain_col
    first = jnp.sum(d_norm, 0, keepdims=True) * (1.0 / 128)
    second = jnp.sum(per_gain * gain_col, 0, keepdims=True) * (1.0 / 128)
    dconv_s[...] = (rstd * (d_norm - first - normed[...] * second)).astype(BF16)
    d_src, d_dst = (lambda p: dconv_s.at[rows16(p), :]), (lambda p: dconv.at[:, lanes(p, 512)])
    start(DCONV, "z", d_src, d_dst)
    dconv[:, lanes(z, 512)] = dconv_s[rows16(z), :]
    gx2_src, gx2_dst = weight_grads(1, G_X2)
    g_x[q] = g_s[:, rows16(q), :]
    gain_sum = jnp.sum(per_gain, 1, keepdims=True)
    gain_s[...] = jnp.sum(jnp.where(diagonal, gain_sum, 0.0), 0, keepdims=True)
    n_src, n_dst = (lambda p: gain_s), (lambda p: gains.at[p])
    start(GAIN, "z", n_src, n_dst)
    gains[z] = gain_s[...]

    branch_s[...] = dot(wo_all, act_h2[...], ((0,), (0,))).astype(BF16)
    branch[:, lanes(z, 512)] = branch_s[rows16(z), :]
    arrive(G_X, "x", gx_src, gx_dst)
    arrive(G_X2, "x", gx2_src, gx2_dst)
    g_xs[...] = jnp.sum(g_x[...].astype(F32), 0).astype(BF16)
    gz_src, gz_dst = (lambda p: g_xs.at[p]), (lambda p: g_z.at[p])
    start(G_Z, "z", gz_src, gz_dst)
    g_z[z] = g_xs[z]
    arrive(DCONV, "z", d_src, d_dst)
    build_cols(dconv, d_cols)
    e1_src, e1_dst = (lambda p: d_cols), (lambda p: d_cols_t.at[p])
    start(D_COLS_Y, "y", e1_src, e1_dst)
    build_rows(dconv, d_rows)
    f1_src, f1_dst = (lambda p: d_rows), (lambda p: d_rows_t.at[p])
    start(D_ROWS_X, "x", f1_src, f1_dst)
    d_cols_t[y] = d_cols[...]
    d_rows_t[q] = d_rows[...]

    spread(dconv, dpad)

    def taps(r, carry):
        for b in range(7):
            moved = roll(dpad[pl.ds(3 + 8 * r, 8)], b - 3, 2)
            for a in range(7):
                sums[a * 7 + b] += jnp.sum(moved * xpad[pl.ds(8 * r + a, 8)], 0)
        return carry

    sums[...] = jnp.zeros((49, 16, 128), F32)
    lax.fori_loop(0, 8, taps, 0)
    small = jnp.zeros((16, 128), F32)
    for tap in range(49):
        small = jnp.where(lane == tap, jnp.sum(sums[tap], 1, keepdims=True), small)
    arrive(GAIN, "z", n_src, n_dst)
    sub = lax.broadcasted_iota(jnp.int32, (16, 128), 0)
    gain_mine = jnp.where(lane == sub + 16 * z, jnp.broadcast_to(jnp.sum(gains[...], 0), (16, 128)), 0.0)
    small = jnp.where(lane == 49, jnp.sum(gain_mine, 1, keepdims=True), small)
    s_y[y] = small
    sy_src, sy_dst = (lambda p: s_y.at[y]), (lambda p: s_y.at[p])
    start(S_Y, "y", sy_src, sy_dst)

    arrive(G_Z, "z", gz_src, gz_dst)
    g_y[y] = jnp.sum(g_z[...].astype(F32), 0)
    gy_src, gy_dst = (lambda p: g_y.at[y]), (lambda p: g_y.at[p])
    start(G_Y, "y", gy_src, gy_dst)
    arrive(D_ROWS_X, "x", f1_src, f1_dst)
    choose_rows(d_rows_t, d_rows_s)
    f2_src, f2_dst = (lambda p: d_rows_s.at[p]), (lambda p: d_rows_g.at[p])
    start(D_ROWS_Y, "y", f2_src, f2_dst)
    arrive(D_COLS_Y, "y", e1_src, e1_dst)
    choose_cols(d_cols_t, d_cols_s)
    e2_src, e2_dst = (lambda p: d_cols_s.at[p]), (lambda p: d_cols_g.at[p])
    start(D_COLS_X, "x", e2_src, e2_dst)
    b_src, b_dst = (lambda p: branch_s.at[rows16(p), :]), (lambda p: branch.at[:, lanes(p, 512)])
    start(BRANCH, "z", b_src, b_dst)
    centre(dpad, True, back_c, 0, 4)
    arrive(S_Y, "y", sy_src, sy_dst)
    s_x[q] = jnp.sum(s_y[...], 0)
    sx_src, sx_dst = (lambda p: s_x.at[q]), (lambda p: s_x.at[p])
    start(S_X, "x", sx_src, sx_dst)
    centre(dpad, True, back_c, 4, N)
    arrive(G_Y, "y", gy_src, gy_dst)
    g_all[q] = jnp.sum(g_y[...], 0)
    ga_src, ga_dst = (lambda p: g_all.at[q]), (lambda p: g_all.at[p])
    start(G_ALL, "x", ga_src, ga_dst)

    arrive(D_ROWS_Y, "y", f2_src, f2_dst)
    arrive(D_COLS_X, "x", e2_src, e2_dst)
    gather_halo(d_rows_s, d_rows_g, d_cols_s, d_cols_g)
    for t, tile_fix in zip((0, 1, 30, 31), fix_rows(True)):
        at = slice(128 * t, 128 * t + 128)
        back_c[:, at] = back_c[:, at] + tile_fix
    fix_cols(True)

    def backward(block, carry):
        for t in range(8):
            at = lanes(8 * block + t)
            whole = back_c[:, at] + jnp.where(edge, roll(fixes[block], 64 - 8 * t, 1), 0.0)
            igrad[:, at] = (cot[:, at].astype(F32) + whole).astype(BF16)
        return carry

    lax.fori_loop(0, 4, backward, 0)
    stores[1].start()

    arrive(BRANCH, "z", b_src, b_dst)

    def write_out(t, carry):
        at = lanes(t, 512)
        kept = mask[:, at].astype(F32)
        out[:, at] = (act[:, at].astype(F32) + kept * branch[:, at].astype(F32)).astype(BF16)
        return carry

    lax.fori_loop(0, 8, write_out, 0)
    stores[0].start()

    settle()
    arrive(S_X, "x", sx_src, sx_dst)
    small = jnp.sum(s_x[...], 0)
    kgrad_out[...] = small[:, 0:49]
    square16 = lax.broadcasted_iota(jnp.int32, (16, 16), 0) == lax.broadcasted_iota(
        jnp.int32, (16, 16), 1
    )
    gain_out[...] = jnp.sum(
        jnp.where(square16, jnp.broadcast_to(small[:, 49:50], (16, 16)), 0.0), 0, keepdims=True
    )
    stores[2].start()
    stores[3].start()
    arrive(G_ALL, "x", ga_src, ga_dst)
    both = g_all[...].reshape(128, 128)
    w_in_out[...] = both[0:64]
    w_out_out[...] = both[64:128]
    stores[4].start()
    stores[5].start()
    settle()
    for store in stores:
        store.wait()


def finish_body(*refs):
    count = (len(refs) - 2) // 3
    arrays, results, held = refs[:count], refs[count : 2 * count], refs[2 * count : 3 * count]
    came, went = refs[-2:]
    loads = [pltpu.make_async_copy(arrays[i], held[i], came.at[i]) for i in range(count)]
    stores = [pltpu.make_async_copy(held[i], results[i], went.at[i]) for i in range(count)]
    for load in loads:
        load.start()
    for load, store in zip(loads, stores):
        load.wait()
        store.start()
    for store in stores:
        store.wait()


def body(activations, cotangent, kernel, gain, w_in, w_out, neighbours, land_mask):
    anywhere = pl.BlockSpec(memory_space=pl.ANY)
    scratch = [
        ((16, 4096), BF16),
        ((16, 4096), BF16),
        ((16, 49), F32),
        ((1, 128), F32),
        ((64, 128), BF16),
        ((64, 128), BF16),
        ((1, 8), jnp.int32),
        ((1, 4096), jnp.int32),
        ((16, 4096), BF16),
        ((16, 4096), BF16),
        ((16, 49), F32),
        ((1, 16), F32),
        ((64, 128), F32),
        ((64, 128), F32),
        ((70, 16, 128), F32),
        ((70, 16, 128), F32),
        ((49, 16, 128), F32),
        ((64, 128), BF16),
        ((64, 128), BF16),
        ((48, 128), BF16),
        ((64, 128), BF16),
        ((N, 64, 128), BF16),
        ((N, 64, 128), BF16),
        ((N, 48, 128), BF16),
        ((N, 64, 128), BF16),
        ((N, N, 8, 128), F32),
        ((N, N, 8, 128), F32),
        ((N, 48, 128), BF16),
        ((N, 80, 128), BF16),
        ((N, 48, 128), BF16),
        ((N, 80, 128), BF16),
        ((N, 48, 128), BF16),
        ((N, 80, 128), BF16),
        ((N, 48, 128), BF16),
        ((N, 80, 128), BF16),
        ((6, 16, 128), F32),
        ((6, 16, 128), F32),
        ((4, 16, 128), F32),
        ((2, 16, 256), F32),
        ((128, 128), F32),
        ((N, 16, 256), F32),
        ((128, 512), F32),
        ((16, 4096), F32),
        ((49, 16, 128), F32),
        ((N, 128, 128), BF16),
        ((16, 4096), BF16),
        ((16, 4096), BF16),
        ((1, 4096), F32),
        ((128, 512), BF16),
        ((N, 1, 512), F32),
        ((128, 512), BF16),
        ((128, 512), F32),
        ((128, 512), BF16),
        ((512, 512), BF16),
        ((512, 512), BF16),
        ((128, 512), BF16),
        ((16, 4096), BF16),
        ((128, 512), BF16),
        ((16, 4096), BF16),
        ((1, 128), F32),
        ((N, 1, 128), F32),
        ((N, 128, 128), BF16),
        ((N, N, 16, 128), BF16),
        ((N, 16, 128), BF16),
        ((N, 16, 128), BF16),
        ((N, 16, 128), F32),
        ((N, 16, 128), F32),
        ((N, 16, 128), F32),
        ((N, 16, 128), F32),
    ]
    shapes = [
        jax.ShapeDtypeStruct((16, 4096), BF16),
        jax.ShapeDtypeStruct((16, 4096), BF16),
        jax.ShapeDtypeStruct((16, 49), F32),
        jax.ShapeDtypeStruct((1, 16), F32),
        jax.ShapeDtypeStruct((64, 128), F32),
        jax.ShapeDtypeStruct((64, 128), F32),
    ]
    results = pl.pallas_call(
        kernel_body,
        out_shape=shapes,
        in_specs=[anywhere] * 8,
        out_specs=[anywhere] * 6,
        scratch_shapes=[pltpu.VMEM(shape, kind) for shape, kind in scratch]
        + [
            pltpu.SemaphoreType.DMA((25, N)),
            pltpu.SemaphoreType.DMA((25, N)),
            pltpu.SemaphoreType.DMA((8,)),
            pltpu.SemaphoreType.DMA((6,)),
        ],
        compiler_params=pltpu.CompilerParams(
            collective_id=0, has_side_effects=True, vmem_limit_bytes=VMEM_LIMIT
        ),
        cost_estimate=pl.CostEstimate(flops=360000000, bytes_accessed=1000000, transcendentals=262144),
        name="block",
    )(
        activations[0], cotangent[0], kernel, gain.reshape(1, 128), w_in.T, w_out, neighbours, land_mask,
    )
    out, igrad, kgrad, ggrad, wigrad, wograd = pl.pallas_call(
        finish_body,
        out_shape=shapes,
        in_specs=[anywhere] * 6,
        out_specs=[anywhere] * 6,
        scratch_shapes=[pltpu.VMEM(result.shape, result.dtype) for result in shapes]
        + [pltpu.SemaphoreType.DMA((6,)), pltpu.SemaphoreType.DMA((6,))],
        compiler_params=pltpu.CompilerParams(vmem_limit_bytes=VMEM_LIMIT),
        name="results",
    )(*results)
    return (out[None], igrad[None], kgrad, ggrad.reshape(16), wigrad.T, wograd)


def solution(mesh):
    placed = (
        P("tile", "chan", None),
        P("tile", "chan", None),
        P("chan", None),
        P(),
        P(None, "chan"),
        P("chan", None),
        P("tile", None),
        P("tile", None),
    )
    return jax.shard_map(
        body,
        mesh=mesh,
        in_specs=placed,
        out_specs=(
            P("tile", "chan", None),
            P("tile", "chan", None),
            P("chan", None),
            P("chan"),
            P(None, "chan"),
            P("chan", None),
        ),
        check_vma=False,
    )
```

```python
import jax
import jax.numpy as jnp
from jax import lax
from jax.experimental import pallas as pl
from jax.experimental.pallas import tpu as pltpu
from jax.sharding import PartitionSpec as P

EPS = 1e-06
N = 8
F32 = jnp.float32
BF16 = jnp.bfloat16
VMEM_LIMIT = 60 * 1024 * 1024

(
    ROWS_X, COLS_Y, ROWS_Y, COLS_X, D_ROWS_X, D_COLS_Y, D_ROWS_Y, D_COLS_X,
    WEIGHTS, MASKED, CONV, MEANS, DCONV, BRANCH, GAIN, G_X, G_X2, G_Z, G_Y, G_ALL, S_Y, S_X,
    FIX_COLS, FIX_ROWS, SIBLING,
) = range(25)


def dot(a, b, dims):
    return lax.dot_general(a, b, (dims, ((), ())), preferred_element_type=F32)


def lanes(t, width=128):
    return pl.ds(pl.multiple_of(t * width, width), width)


def rows16(p):
    return pl.ds(pl.multiple_of(p * 16, 16), 16)


def kernel_body(
    act_h, cot_h, ker_h, gain_h, w_in_h, w_out_h, nbr_h, mask_h,
    out_h, igrad_h, kgrad_h, ggrad_h, w_in_grad_h, w_out_grad_h,
    act, cot, ker, gain, w_in, w_out, nbr, mask,
    out, igrad, kgrad_out, gain_out, w_in_out, w_out_out,
    xpad, dpad, wb, rows, cols, d_rows, d_cols,
    rows_t, cols_t, d_rows_t, d_cols_t, row_masks, col_masks,
    rows_s, cols_s, d_rows_s, d_cols_s, rows_g, cols_g, d_rows_g, d_cols_g,
    outers, sides, fixes, row_fix, fix_g, row_fix_g, added_in, back_c, sums,
    weights, masked, conv_r, means, convs, mean_all, dz, normed, feats, act_h2, dpre_h,
    dconv_s, dconv, branch_s, branch, gain_s, gains, g_s, g_x, g_xs, g_z, g_y, g_all, s_y, s_x,
    ssem, rsem, lsem, osem,
):
    tile = lax.axis_index("tile")
    z = lax.axis_index("chan")
    y = tile // N
    q = lax.rem(tile, N)
    mine = {"y": y, "x": q, "z": z}

    def device(group, p):
        if group == "y":
            return (p * N + q, z)
        if group == "x":
            return (y * N + p, z)
        return (tile, p)

    def copy(stage, group, src, dst, to, slot):
        return pltpu.make_async_remote_copy(
            src_ref=src,
            dst_ref=dst,
            send_sem=ssem.at[stage, to],
            recv_sem=rsem.at[stage, slot],
            device_id=device(group, to),
            device_id_type=pl.DeviceIdType.MESH,
        )

    def peers(group, step):
        for offset in (4, 3, 5, 2, 6, 1, 7):
            step((mine[group] + offset) & (N - 1))

    sent = []

    def start(stage, group, src, dst):
        me = mine[group]
        peers(group, lambda p: copy(stage, group, src(p), dst(me), p, me).start())
        sent.append((stage, group, src, dst))

    def arrive(stage, group, src, dst):
        peers(group, lambda p: copy(stage, group, src(p), dst(p), p, p).wait_recv())

    def settle():
        for stage, group, src, dst in sent:
            me = mine[group]
            peers(group, lambda p: copy(stage, group, src(p), dst(me), p, me).wait_send())
        sent.clear()

    lane = lax.broadcasted_iota(jnp.int32, (16, 128), 1)
    lane1 = lax.broadcasted_iota(jnp.int32, (1, 1, 128), 2)
    low = lane < 64
    rest = lane & 63
    edge = (rest < 3) | (rest >= 61)
    beside = ((lane >= 64) & (lane < 67)) | (lane >= 125)

    def window_in(index, members):
        found = index < 0
        for member in members:
            found = found | (index == member)
        return found

    def pair(ref, t):
        return ref[:, lanes(t)].astype(F32)

    def roll(x, shift, axis):
        shift = shift % 128
        return x if shift == 0 else pltpu.roll(x, shift, axis)

    inputs = [
        (act_h, act), (nbr_h, nbr), (cot_h, cot), (mask_h, mask),
        (w_in_h, w_in), (w_out_h, w_out), (ker_h, ker), (gain_h, gain),
    ]
    loads = [pltpu.make_async_copy(src, dst, lsem.at[i]) for i, (src, dst) in enumerate(inputs)]
    results = [
        (out, out_h), (igrad, igrad_h), (kgrad_out, kgrad_h), (gain_out, ggrad_h),
        (w_in_out, w_in_grad_h), (w_out_out, w_out_grad_h),
    ]
    stores = [pltpu.make_async_copy(src, dst, osem.at[i]) for i, (src, dst) in enumerate(results)]

    barrier = pltpu.get_barrier_semaphore()
    for group in ("y", "x", "z"):
        peers(
            group,
            lambda p, group=group: pl.semaphore_signal(
                barrier, inc=1, device_id=device(group, p), device_id_type=pl.DeviceIdType.MESH
            ),
        )
    for load in loads:
        load.start()

    def build_rows(src, dst):
        dst[0:16, :] = src[:, 0:128]
        dst[16:32, :] = jnp.where(low, pair(src, 1), pair(src, 30)).astype(BF16)
        dst[32:48, :] = src[:, 3968:4096]

    def build_cols(src, dst):
        for block in range(4):
            total = jnp.zeros((16, 128), F32)
            for t in range(8):
                total = total + roll(jnp.where(edge, pair(src, block * 8 + t), 0.0), 8 * t, 1)
            dst[16 * block : 16 * block + 16, :] = total.astype(BF16)

    loads[0].wait()
    build_cols(act, cols)
    build_rows(act, rows)
    loads[1].wait()
    eight = lax.broadcasted_iota(jnp.int32, (16, 8), 0) == lax.broadcasted_iota(jnp.int32, (16, 8), 1)
    listed = jnp.sum(
        jnp.where(eight, jnp.broadcast_to(nbr[...].astype(F32), (16, 8)), 0.0), 1, keepdims=True
    )
    listed = jnp.broadcast_to(listed, (16, 128)).astype(BF16)
    rows[48:64, :] = listed
    for k in range(8):
        spare = jnp.broadcast_to(nbr[0:1, k : k + 1].astype(F32), (16, 128)).astype(BF16)
        cols[0:16, :] = jnp.where(lane == 8 * k + 3, spare, cols[0:16, :])

    pl.semaphore_wait(barrier, 3 * (N - 1))
    c1_src, c1_dst = (lambda p: cols), (lambda p: cols_t.at[p])
    start(COLS_Y, "y", c1_src, c1_dst)
    r1_src, r1_dst = (lambda p: rows), (lambda p: rows_t.at[p])
    start(ROWS_X, "x", r1_src, r1_dst)
    cols_t[y] = cols[...]
    rows_t[q] = rows[...]

    for load in loads[2:]:
        load.wait()
    core = q & 1
    mine_half = pl.ds(pl.multiple_of(64 * core, 64), 64)
    weights[z, mine_half, :] = jnp.where(core == 0, w_in[...], w_out[...])
    w_src, w_dst = (lambda p: weights.at[z, mine_half]), (lambda p: weights.at[p, mine_half])
    start(WEIGHTS, "z", w_src, w_dst)

    def sibling(half, slot):
        part = weights.at[:, half]
        return copy(SIBLING, "x", part, part, q ^ 1, slot)

    def mask_cot(t, carry):
        kept = mask[:, lanes(t, 512)].astype(F32)
        masked[:, lanes(t, 512)] = (cot[:, lanes(t, 512)].astype(F32) * kept).astype(BF16)
        return carry

    lax.fori_loop(0, 8, mask_cot, 0)
    m_src, m_dst = (lambda p: masked.at[:, lanes(p, 512)]), (lambda p: dz.at[rows16(p), :])
    start(MASKED, "z", m_src, m_dst)
    dz[rows16(z), :] = masked[:, lanes(z, 512)]

    for tap in range(49):
        wb[tap] = jnp.broadcast_to(ker[:, tap : tap + 1], (16, 128))

    def spread(src, dst):
        def some(block, carry):
            for u in range(8):
                both = pair(src, 8 * block + u)
                dst[3 + 16 * block + 2 * u] = jnp.where(low, both, 0.0)
                dst[4 + 16 * block + 2 * u] = jnp.where(low, roll(both, 64, 1), 0.0)
            return carry

        for row in (0, 1, 2, 67, 68, 69):
            dst[row] = jnp.zeros((16, 128), F32)
        lax.fori_loop(0, 4, some, 0)

    spread(act, xpad)

    def filtered(src, flip, r):
        total = None
        for b in range(7):
            part = None
            for a in range(7):
                tap = (6 - a) * 7 + 6 - b if flip else a * 7 + b
                term = wb[tap][None] * src[pl.ds(8 * r + a, 8)]
                part = term if part is None else part + term
            part = roll(part, 3 - b, 2)
            total = part if total is None else total + part
        return [jnp.where(low, total[2 * u], roll(total[2 * u + 1], 64, 1)) for u in range(4)]

    def centre(src, flip, dst):
        def some(r, carry):
            tiles = filtered(src, flip, r)
            for u in range(4):
                dst[:, lanes(4 * r + u)] = tiles[u]
            return carry

        lax.fori_loop(0, N, some, 0)

    def forward(r, carry):
        tiles = filtered(xpad, False, r)
        for u in range(4):
            mean = jnp.sum(tiles[u], 0, keepdims=True) * (1.0 / 16)
            conv_r[:, lanes(4 * r + u)] = (tiles[u] - mean).astype(BF16)
            means[:, lanes(4 * r + u)] = mean
        return carry

    lax.fori_loop(0, N, forward, 0)
    c_src, c_dst = (lambda p: conv_r.at[:, lanes(p, 512)]), (lambda p: convs.at[rows16(p), :])
    a_src, a_dst = (lambda p: means.at[:, lanes(p, 512)]), (lambda p: mean_all.at[p])
    start(CONV, "z", c_src, c_dst)
    start(MEANS, "z", a_src, a_dst)
    convs[rows16(z), :] = conv_r[:, lanes(z, 512)]
    mean_all[z] = means[:, lanes(z, 512)]

    index4 = lane1 // 4
    odd = (index4 & 1) == 1
    in_top = window_in(index4, (0, 15, 16, 31, 2, 17))
    in_bottom = window_in(index4, (28, 11, 14, 29, 30, 13))

    def make_col_masks(d, carry):
        number = (y * N + d).astype(F32)
        near = (cols_t[:, 0:16, :].astype(F32)[:, 0:1, :] == number).astype(F32)
        m = [jnp.broadcast_to(near[:, :, 8 * k + 3 : 8 * k + 4], (N, 1, 128)) for k in range(8)]
        col_masks[d, :, 0:1, :] = jnp.where(odd, m[4], m[3])
        col_masks[d, :, 1:2, :] = jnp.where(
            in_top, jnp.where(odd, m[2], m[0]), jnp.where(in_bottom, jnp.where(odd, m[7], m[5]), 0.0)
        )
        return carry

    def make_row_masks(d, carry):
        number = (d * N + q).astype(F32)
        near = (rows_t[:, 48:64, :].astype(F32) == number).astype(F32)
        m = [near[:, k : k + 1, :] for k in range(8)]
        row_masks[d, :, 0:1, :] = m[1]
        row_masks[d, :, 1:2, :] = jnp.where(lane1 < 64, m[1], m[6])
        row_masks[d, :, 2:3, :] = m[6]
        return carry

    def choose_rows(src, dst):
        def one(d, carry):
            for part in range(3):
                block = src[:, 16 * part : 16 * part + 16, :].astype(F32)
                total = jnp.sum(row_masks[d, :, part : part + 1, :] * block, 0)
                dst[d, 16 * part : 16 * part + 16, :] = total.astype(BF16)
            return carry

        lax.fori_loop(0, N, one, 0, unroll=2)

    def choose_cols(src, dst):
        def one(d, carry):
            for part in range(4):
                block = src[:, 16 * part : 16 * part + 16, :].astype(F32)
                total = jnp.sum(col_masks[d, :, 0:1, :] * block, 0)
                dst[d, 16 * part : 16 * part + 16, :] = total.astype(BF16)
            block = jnp.where(in_bottom, src[:, 48:64, :].astype(F32), src[:, 0:16, :].astype(F32))
            dst[d, 64:80, :] = jnp.sum(col_masks[d, :, 1:2, :] * block, 0).astype(BF16)
            return carry

        lax.fori_loop(0, N, one, 0, unroll=2)

    def added(me, own, got, i):
        total = own[me, 16 * i : 16 * i + 16, :].astype(F32)
        for j in range(1, N):
            total = total + got[lax.rem(me + j, N), 16 * i : 16 * i + 16, :].astype(F32)
        return total

    block8, in8 = lane1 // 8, lane1 & 7
    place = jnp.where(in8 < 4, (block8 + 8) & 15, (block8 + 1) & 15)
    half, step = jnp.where(place < 8, 1, 0), place & 7

    def gather_halo(own_rows, got_rows, own_cols, got_cols):
        top, mid, end = [added(y, own_rows, got_rows, i) for i in range(3)]
        corner = added(q, own_cols, got_cols, 4)
        centres = (roll(mid, 64, 1), end, roll(end, 64, 1), top, roll(top, 64, 1), mid)
        for i, shift in enumerate((80, 8, 72, 64, 0, 56)):
            outers[i] = jnp.where(low, centres[i], jnp.where(beside, roll(corner, shift, 1), 0.0))
        sides[0] = jnp.zeros((16, 128), F32)
        sides[5] = jnp.zeros((16, 128), F32)
        for block in range(4):
            sides[1 + block] = added(q, own_cols, got_cols, block)

    def fill_pad(dst):
        for i, row in enumerate((0, 1, 2, 67, 68, 69)):
            dst[row] = outers[i]
        for block in range(4):
            side = sides[1 + block]
            for t in range(8):
                for o in range(2):
                    row = 3 + 16 * block + 2 * t + o
                    near = roll(side, 64 * (1 - o) - 8 * t, 1)
                    dst[row] = dst[row] + jnp.where(beside, near, 0.0)

    def fix_rows(flip):
        def fixed(pieces):
            total = None
            for b in range(7):
                part = None
                for a, i in pieces:
                    tap = (6 - a) * 7 + 6 - b if flip else a * 7 + b
                    term = wb[tap] * outers[i]
                    part = term if part is None else part + term
                part = roll(part, 3 - b, 1)
                total = part if total is None else total + part
            return total

        tops = [fixed([(a, i + a) for a in range(3 - i)]) for i in range(3)]
        ends = [fixed([(6 - i + m, 3 + m) for m in range(i + 1)]) for i in range(3)]
        zero = jnp.zeros((16, 128), F32)
        return [
            jnp.where(low, lower, roll(upper, 64, 1))
            for lower, upper in ((tops[0], tops[1]), (tops[2], zero), (zero, ends[0]), (ends[1], ends[2]))
        ]

    def fix_cols(flip):
        for first in (0, 2):
            parts = [None] * 7
            for a in range(7):
                by = a - 3
                moved = sides[first + 1 : first + 3]
                if by:
                    moved = jnp.zeros((2, 16, 128), F32)
                    for o in range(2):
                        up = (o + by) // 2
                        other = (o + by) - 2 * up
                        for over in (-1, 0, 1):
                            if over * up < 0 or (over and not up):
                                continue
                            fits = (half == o) & (step + up >= 8 * over) & (step + up < 8 * over + 8)
                            source = sides[first + 1 + over : first + 3 + over]
                            shift = -8 * (up - 8 * over + 8 * (o - other))
                            moved = jnp.where(fits, roll(source, shift, 2), moved)
                for b in (0, 1, 2, 4, 5, 6):
                    tap = (6 - a) * 7 + 6 - b if flip else a * 7 + b
                    term = wb[tap][None] * moved
                    parts[b] = term if parts[b] is None else parts[b] + term
            total = jnp.zeros((2, 16, 128), F32)
            for b in (0, 1, 2, 4, 5, 6):
                lands = in8 < 3 - b if b < 3 else in8 > 10 - b
                total = total + jnp.where(lands, roll(parts[b], 3 - b, 2), 0.0)
            fixes[first : first + 2] = total

    arrive(ROWS_X, "x", r1_src, r1_dst)
    lax.fori_loop(0, N, make_row_masks, 0, unroll=2)
    choose_rows(rows_t, rows_s)
    r2_src, r2_dst = (lambda p: rows_s.at[p]), (lambda p: rows_g.at[p])
    start(ROWS_Y, "y", r2_src, r2_dst)
    arrive(COLS_Y, "y", c1_src, c1_dst)
    lax.fori_loop(0, N, make_col_masks, 0, unroll=2)
    choose_cols(cols_t, cols_s)
    c2_src, c2_dst = (lambda p: cols_s.at[p]), (lambda p: cols_g.at[p])
    start(COLS_X, "x", c2_src, c2_dst)
    arrive(WEIGHTS, "z", w_src, w_dst)
    sibling(mine_half, q).start()
    arrive(ROWS_Y, "y", r2_src, r2_dst)
    arrive(COLS_X, "x", c2_src, c2_dst)
    gather_halo(rows_s, rows_g, cols_s, cols_g)
    fix_cols(False)
    k_src, k_dst = (lambda p: fixes.at[p // 2]), (lambda p: fix_g.at[rows16(p), :])
    start(FIX_COLS, "z", k_src, k_dst)
    for i, tile_fix in enumerate(fix_rows(False)):
        row_fix[i // 2, :, 128 * (i % 2) : 128 * (i % 2) + 128] = tile_fix

    def row_copy(end, slot):
        return copy(FIX_ROWS, "z", row_fix.at[end], row_fix_g.at[slot], (N - 1) * end, slot)

    for end in range(2):

        @pl.when(z != (N - 1) * end)
        def _():
            row_copy(end, z).start()

    fill_pad(xpad)
    settle()
    for end in range(2):

        @pl.when(z != (N - 1) * end)
        def _():
            row_copy(end, z).wait_send()

    sibling(mine_half, q).wait_send()
    sibling(pl.ds(pl.multiple_of(64 - 64 * core, 64), 64), q ^ 1).wait_recv()
    fix_g[rows16(z), :] = fixes[z // 2]
    arrive(CONV, "z", c_src, c_dst)
    arrive(MEANS, "z", a_src, a_dst)
    arrive(FIX_COLS, "z", k_src, k_dst)
    turned = pltpu.roll(fix_g[...], lax.rem(128 - 32 * (z & 1), 128), 1)
    border = edge[0:1, :]
    for u in range(4):
        added_in[:, 128 * u : 128 * u + 128] = jnp.where(border, roll(turned, 64 - 8 * u, 1), 0.0)
    for end in range(2):

        @pl.when(z == (N - 1) * end)
        def _():
            row_fix_g[z] = row_fix[end]
            peers("z", lambda p: row_copy(end, p).wait_recv())
            at = slice(256 * end, 256 * end + 256)
            added_in[:, at] = added_in[:, at] + row_fix_g[...].reshape(128, 256)

    local = mean_all[...]
    extra = added_in[...]
    mean = jnp.sum(local, 0) * (1.0 / N) + jnp.sum(extra, 0, keepdims=True) * (1.0 / 128)
    centred = (convs[...].astype(F32) + extra).reshape(N, 16, 512) + (local - mean[None])
    centred = centred.reshape(128, 512)
    rstd = lax.rsqrt(jnp.sum(centred * centred, 0, keepdims=True) * (1.0 / 128) + EPS)
    normed[...] = centred * rstd
    diagonal = lax.broadcasted_iota(jnp.int32, (128, 128), 0) == lax.broadcasted_iota(
        jnp.int32, (128, 128), 1
    )
    gain_col = jnp.sum(jnp.where(diagonal, jnp.broadcast_to(gain[...], (128, 128)), 0.0), 1, keepdims=True)
    feats[...] = (normed[...] * gain_col).astype(BF16)
    arrive(MASKED, "z", m_src, m_dst)

    def hidden(g, carry):
        wi = weights[pl.ds(2 * g, 2), 0:64, :].reshape(128, 128)
        wo = weights[pl.ds(2 * g, 2), 64:128, :].reshape(128, 128)
        pre = dot(wi, feats[...], ((1,), (0,)))
        square = pre * pre
        bend = jnp.tanh(0.7978845608 * pre * (1.0 + 0.044715 * square))
        half = 0.5 + 0.5 * bend
        act_h2[lanes(g), :] = (pre * half).astype(BF16)
        slope = half + (0.5 * 0.7978845608) * pre * (1.0 - bend * bend) * (
            1.0 + (3.0 * 0.044715) * square
        )
        d_act = dot(wo, dz[...], ((1,), (0,)))
        dpre_h[lanes(g), :] = (d_act * slope).astype(BF16)
        return carry

    def weight_grads(part, stage):
        units, groups = slice(256 * part, 256 * part + 256), pl.ds(4 * part, 4)
        g_s[groups, 0:64, :] = dot(dpre_h[units, :], feats[...], ((1,), (1,))).astype(BF16).reshape(4, 64, 128)
        g_s[groups, 64:128, :] = dot(act_h2[units, :], dz[...], ((1,), (1,))).astype(BF16).reshape(4, 64, 128)
        src, dst = (lambda p: g_s.at[groups, rows16(p), :]), (lambda p: g_x.at[p, groups])
        start(stage, "x", src, dst)
        return src, dst

    lax.fori_loop(0, 2, hidden, 0)
    gx_src, gx_dst = weight_grads(0, G_X)
    lax.fori_loop(2, 4, hidden, 0)
    wi_all = weights[:, 0:64, :].reshape(512, 128)
    wo_all = weights[:, 64:128, :].reshape(512, 128)
    d_feat = dot(wi_all, dpre_h[...], ((0,), (0,)))
    per_gain = d_feat * normed[...]
    d_norm = d_feat * gain_col
    first = jnp.sum(d_norm, 0, keepdims=True) * (1.0 / 128)
    second = jnp.sum(per_gain * gain_col, 0, keepdims=True) * (1.0 / 128)
    dconv_s[...] = (rstd * (d_norm - first - normed[...] * second)).astype(BF16)
    d_src, d_dst = (lambda p: dconv_s.at[rows16(p), :]), (lambda p: dconv.at[:, lanes(p, 512)])
    start(DCONV, "z", d_src, d_dst)
    dconv[:, lanes(z, 512)] = dconv_s[rows16(z), :]
    gx2_src, gx2_dst = weight_grads(1, G_X2)
    g_x[q] = g_s[:, rows16(q), :]
    gain_sum = jnp.sum(per_gain, 1, keepdims=True)
    gain_s[...] = jnp.sum(jnp.where(diagonal, gain_sum, 0.0), 0, keepdims=True)
    n_src, n_dst = (lambda p: gain_s), (lambda p: gains.at[p])
    start(GAIN, "z", n_src, n_dst)
    gains[z] = gain_s[...]

    branch_s[...] = dot(wo_all, act_h2[...], ((0,), (0,))).astype(BF16)
    branch[:, lanes(z, 512)] = branch_s[rows16(z), :]
    arrive(G_X, "x", gx_src, gx_dst)
    arrive(G_X2, "x", gx2_src, gx2_dst)
    g_xs[...] = jnp.sum(g_x[...].astype(F32), 0).astype(BF16)
    gz_src, gz_dst = (lambda p: g_xs.at[p]), (lambda p: g_z.at[p])
    start(G_Z, "z", gz_src, gz_dst)
    g_z[z] = g_xs[z]
    arrive(DCONV, "z", d_src, d_dst)
    build_cols(dconv, d_cols)
    e1_src, e1_dst = (lambda p: d_cols), (lambda p: d_cols_t.at[p])
    start(D_COLS_Y, "y", e1_src, e1_dst)
    build_rows(dconv, d_rows)
    f1_src, f1_dst = (lambda p: d_rows), (lambda p: d_rows_t.at[p])
    start(D_ROWS_X, "x", f1_src, f1_dst)
    d_cols_t[y] = d_cols[...]
    d_rows_t[q] = d_rows[...]

    spread(dconv, dpad)

    def taps(r, carry):
        for b in range(7):
            moved = roll(dpad[pl.ds(3 + 8 * r, 8)], b - 3, 2)
            for a in range(7):
                sums[a * 7 + b] += jnp.sum(moved * xpad[pl.ds(8 * r + a, 8)], 0)
        return carry

    sums[...] = jnp.zeros((49, 16, 128), F32)
    lax.fori_loop(0, 8, taps, 0)
    small = jnp.zeros((16, 128), F32)
    for tap in range(49):
        small = jnp.where(lane == tap, jnp.sum(sums[tap], 1, keepdims=True), small)
    arrive(GAIN, "z", n_src, n_dst)
    sub = lax.broadcasted_iota(jnp.int32, (16, 128), 0)
    gain_mine = jnp.where(lane == sub + 16 * z, jnp.broadcast_to(jnp.sum(gains[...], 0), (16, 128)), 0.0)
    small = jnp.where(lane == 49, jnp.sum(gain_mine, 1, keepdims=True), small)
    s_y[y] = small
    sy_src, sy_dst = (lambda p: s_y.at[y]), (lambda p: s_y.at[p])
    start(S_Y, "y", sy_src, sy_dst)

    arrive(G_Z, "z", gz_src, gz_dst)
    g_y[y] = jnp.sum(g_z[...].astype(F32), 0)
    gy_src, gy_dst = (lambda p: g_y.at[y]), (lambda p: g_y.at[p])
    start(G_Y, "y", gy_src, gy_dst)
    arrive(D_ROWS_X, "x", f1_src, f1_dst)
    choose_rows(d_rows_t, d_rows_s)
    f2_src, f2_dst = (lambda p: d_rows_s.at[p]), (lambda p: d_rows_g.at[p])
    start(D_ROWS_Y, "y", f2_src, f2_dst)
    arrive(D_COLS_Y, "y", e1_src, e1_dst)
    choose_cols(d_cols_t, d_cols_s)
    e2_src, e2_dst = (lambda p: d_cols_s.at[p]), (lambda p: d_cols_g.at[p])
    start(D_COLS_X, "x", e2_src, e2_dst)
    b_src, b_dst = (lambda p: branch_s.at[rows16(p), :]), (lambda p: branch.at[:, lanes(p, 512)])
    start(BRANCH, "z", b_src, b_dst)
    centre(dpad, True, back_c)
    arrive(S_Y, "y", sy_src, sy_dst)
    s_x[q] = jnp.sum(s_y[...], 0)
    sx_src, sx_dst = (lambda p: s_x.at[q]), (lambda p: s_x.at[p])
    start(S_X, "x", sx_src, sx_dst)
    arrive(G_Y, "y", gy_src, gy_dst)
    g_all[q] = jnp.sum(g_y[...], 0)
    ga_src, ga_dst = (lambda p: g_all.at[q]), (lambda p: g_all.at[p])
    start(G_ALL, "x", ga_src, ga_dst)

    arrive(D_ROWS_Y, "y", f2_src, f2_dst)
    arrive(D_COLS_X, "x", e2_src, e2_dst)
    gather_halo(d_rows_s, d_rows_g, d_cols_s, d_cols_g)
    for t, tile_fix in zip((0, 1, 30, 31), fix_rows(True)):
        at = slice(128 * t, 128 * t + 128)
        back_c[:, at] = back_c[:, at] + tile_fix
    fix_cols(True)

    def backward(block, carry):
        for t in range(8):
            at = lanes(8 * block + t)
            whole = back_c[:, at] + jnp.where(edge, roll(fixes[block], 64 - 8 * t, 1), 0.0)
            igrad[:, at] = (cot[:, at].astype(F32) + whole).astype(BF16)
        return carry

    lax.fori_loop(0, 4, backward, 0)
    stores[1].start()

    arrive(BRANCH, "z", b_src, b_dst)

    def write_out(t, carry):
        at = lanes(t, 512)
        kept = mask[:, at].astype(F32)
        out[:, at] = (act[:, at].astype(F32) + kept * branch[:, at].astype(F32)).astype(BF16)
        return carry

    lax.fori_loop(0, 8, write_out, 0)
    stores[0].start()

    settle()
    arrive(S_X, "x", sx_src, sx_dst)
    small = jnp.sum(s_x[...], 0)
    kgrad_out[...] = small[:, 0:49]
    square16 = lax.broadcasted_iota(jnp.int32, (16, 16), 0) == lax.broadcasted_iota(
        jnp.int32, (16, 16), 1
    )
    gain_out[...] = jnp.sum(
        jnp.where(square16, jnp.broadcast_to(small[:, 49:50], (16, 16)), 0.0), 0, keepdims=True
    )
    stores[2].start()
    stores[3].start()
    arrive(G_ALL, "x", ga_src, ga_dst)
    both = g_all[...].reshape(128, 128)
    w_in_out[...] = both[0:64]
    w_out_out[...] = both[64:128]
    stores[4].start()
    stores[5].start()
    settle()
    for store in stores:
        store.wait()


def finish_body(*refs):
    count = (len(refs) - 2) // 3
    arrays, results, held = refs[:count], refs[count : 2 * count], refs[2 * count : 3 * count]
    came, went = refs[-2:]
    loads = [pltpu.make_async_copy(arrays[i], held[i], came.at[i]) for i in range(count)]
    stores = [pltpu.make_async_copy(held[i], results[i], went.at[i]) for i in range(count)]
    for load in loads:
        load.start()
    for load, store in zip(loads, stores):
        load.wait()
        store.start()
    for store in stores:
        store.wait()


def body(activations, cotangent, kernel, gain, w_in, w_out, neighbours, land_mask):
    anywhere = pl.BlockSpec(memory_space=pl.ANY)
    scratch = [
        ((16, 4096), BF16),
        ((16, 4096), BF16),
        ((16, 49), F32),
        ((1, 128), F32),
        ((64, 128), BF16),
        ((64, 128), BF16),
        ((1, 8), jnp.int32),
        ((1, 4096), jnp.int32),
        ((16, 4096), BF16),
        ((16, 4096), BF16),
        ((16, 49), F32),
        ((1, 16), F32),
        ((64, 128), F32),
        ((64, 128), F32),
        ((70, 16, 128), F32),
        ((70, 16, 128), F32),
        ((49, 16, 128), F32),
        ((64, 128), BF16),
        ((64, 128), BF16),
        ((48, 128), BF16),
        ((64, 128), BF16),
        ((N, 64, 128), BF16),
        ((N, 64, 128), BF16),
        ((N, 48, 128), BF16),
        ((N, 64, 128), BF16),
        ((N, N, 8, 128), F32),
        ((N, N, 8, 128), F32),
        ((N, 48, 128), BF16),
        ((N, 80, 128), BF16),
        ((N, 48, 128), BF16),
        ((N, 80, 128), BF16),
        ((N, 48, 128), BF16),
        ((N, 80, 128), BF16),
        ((N, 48, 128), BF16),
        ((N, 80, 128), BF16),
        ((6, 16, 128), F32),
        ((6, 16, 128), F32),
        ((4, 16, 128), F32),
        ((2, 16, 256), F32),
        ((128, 128), F32),
        ((N, 16, 256), F32),
        ((128, 512), F32),
        ((16, 4096), F32),
        ((49, 16, 128), F32),
        ((N, 128, 128), BF16),
        ((16, 4096), BF16),
        ((16, 4096), BF16),
        ((1, 4096), F32),
        ((128, 512), BF16),
        ((N, 1, 512), F32),
        ((128, 512), BF16),
        ((128, 512), F32),
        ((128, 512), BF16),
        ((512, 512), BF16),
        ((512, 512), BF16),
        ((128, 512), BF16),
        ((16, 4096), BF16),
        ((128, 512), BF16),
        ((16, 4096), BF16),
        ((1, 128), F32),
        ((N, 1, 128), F32),
        ((N, 128, 128), BF16),
        ((N, N, 16, 128), BF16),
        ((N, 16, 128), BF16),
        ((N, 16, 128), BF16),
        ((N, 16, 128), F32),
        ((N, 16, 128), F32),
        ((N, 16, 128), F32),
        ((N, 16, 128), F32),
    ]
    shapes = [
        jax.ShapeDtypeStruct((16, 4096), BF16),
        jax.ShapeDtypeStruct((16, 4096), BF16),
        jax.ShapeDtypeStruct((16, 49), F32),
        jax.ShapeDtypeStruct((1, 16), F32),
        jax.ShapeDtypeStruct((64, 128), F32),
        jax.ShapeDtypeStruct((64, 128), F32),
    ]
    results = pl.pallas_call(
        kernel_body,
        out_shape=shapes,
        in_specs=[anywhere] * 8,
        out_specs=[anywhere] * 6,
        scratch_shapes=[pltpu.VMEM(shape, kind) for shape, kind in scratch]
        + [
            pltpu.SemaphoreType.DMA((25, N)),
            pltpu.SemaphoreType.DMA((25, N)),
            pltpu.SemaphoreType.DMA((8,)),
            pltpu.SemaphoreType.DMA((6,)),
        ],
        compiler_params=pltpu.CompilerParams(
            collective_id=0, has_side_effects=True, vmem_limit_bytes=VMEM_LIMIT
        ),
        cost_estimate=pl.CostEstimate(flops=360000000, bytes_accessed=1000000, transcendentals=262144),
        name="block",
    )(
        activations[0], cotangent[0], kernel, gain.reshape(1, 128), w_in.T, w_out, neighbours, land_mask,
    )
    out, igrad, kgrad, ggrad, wigrad, wograd = pl.pallas_call(
        finish_body,
        out_shape=shapes,
        in_specs=[anywhere] * 6,
        out_specs=[anywhere] * 6,
        scratch_shapes=[pltpu.VMEM(result.shape, result.dtype) for result in shapes]
        + [pltpu.SemaphoreType.DMA((6,)), pltpu.SemaphoreType.DMA((6,))],
        compiler_params=pltpu.CompilerParams(vmem_limit_bytes=VMEM_LIMIT),
        name="results",
    )(*results)
    return (out[None], igrad[None], kgrad, ggrad.reshape(16), wigrad.T, wograd)


def solution(mesh):
    placed = (
        P("tile", "chan", None),
        P("tile", "chan", None),
        P("chan", None),
        P(),
        P(None, "chan"),
        P("chan", None),
        P("tile", None),
        P("tile", None),
    )
    return jax.shard_map(
        body,
        mesh=mesh,
        in_specs=placed,
        out_specs=(
            P("tile", "chan", None),
            P("tile", "chan", None),
            P("chan", None),
            P("chan"),
            P(None, "chan"),
            P("chan", None),
        ),
        check_vma=False,
    )
```
